512 devices in a mesh: pipe: 32 (over x, z_lo), tp: 16 (over y, z_hi, core).
Axes of the slice: x: 4, y: 4, z: 16 (z_hi: 2, z_lo: 8; z = z_hi * 8 + z_lo), core: 2. Of those that a mesh axis runs over, the one named last changes fastest.
Arguments:
- mixed_fwd: bfloat16 [32, 128, 8192], P('pipe', None, 'tp'), may hold values from -6 to 6
- resid_fwd: bfloat16 [32, 128, 4096], P('pipe', 'tp'), may hold values from -6 to 6
- weight_vals: bfloat16 [32, 8192, 4096], P('pipe', 'tp'), as said below
- weight_exps: int32 [32, 256], P('pipe', 'tp'), may hold values from 117 to 121
- inner_x: bfloat16 [32, 128, 8192], P('pipe', None, 'tp'), may hold values from -6 to 6
- inner_z: bfloat16 [32, 128, 8192], P('pipe', None, 'tp'), may hold values from -6 to 6
- proj_b: bfloat16 [32, 128, 2048], P('pipe', None, 'tp'), may hold values from -2 to 2
- proj_c: bfloat16 [32, 128, 2048], P('pipe', None, 'tp'), may hold values from -2 to 2
- step_raw: bfloat16 [32, 128, 128], P('pipe', None, 'tp'), may hold values from -3 to 9
- step_bias: float32 [32, 128], P('pipe', 'tp'), may hold values from -0.5 to 0.5
- decay_log: float32 [32, 128], P('pipe', 'tp'), as said below
- head_skip_weight: float32 [32, 128], P('pipe', 'tp'), may hold values from 0.5 to 1.5
- norm_gain: float32 [32, 8192], P('pipe', 'tp'), may hold values from 0.25 to 1.75
- upstream: bfloat16 [32, 128, 4096], P('pipe', 'tp'), may hold values from -6 to 6
Outputs:
- arriving: bfloat16 [32, 128, 4096], P('pipe', 'tp')
- grad_x: bfloat16 [32, 128, 8192], P('pipe', None, 'tp')
- grad_z: bfloat16 [32, 128, 8192], P('pipe', None, 'tp')
- grad_b: bfloat16 [32, 128, 2048], P('pipe', None, 'tp')
- grad_c: bfloat16 [32, 128, 2048], P('pipe', None, 'tp')
- grad_step: bfloat16 [32, 128, 128], P('pipe', None, 'tp')
- grad_bias: float32 [32, 128], P('pipe', 'tp')
- grad_decay: float32 [32, 128], P('pipe', 'tp')
- grad_skip: float32 [32, 128], P('pipe', 'tp')
- grad_gain: float32 [32, 8192], P('pipe', 'tp')
The draws below stay inside these ranges and needn't reach their ends.
Inputs may be any that keep to these rules, and one draw needn't show every extreme that they name: `weight_vals`: every entry is plus or minus (1 + m / 8) times 2 ** k with whole m from 0 to 7 and k from -2 to 0. exp(decay_log) * 128 lies between 1 and 13.
All inputs are finite; a program needn't handle non-finite values.
Results may differ from the reference program's by a relative error of at most 0.015.
Values may be sent and summed in bfloat16 or wider, within the bound.
A program may use at most 64 MiB of HBM per device.

```python
import jax
import jax.numpy as jnp
from jax import lax

D = 4096
STATE = 128
SCALE_BLOCK = 32
BATCH_TOKENS = 128
D_INNER = 8192
HEADS = 128
GROUPS = 16
N_PIPE = 32


def draw_weight_vals(key, part):
    key = jax.random.fold_in(key, 11)
    drawn_code = jax.random.randint(key, (N_PIPE, D_INNER, D), 0, 48)
    sign_bit = drawn_code % 2
    mantissa = drawn_code // 2 % 8
    exponent = drawn_code // 16
    magnitude = (1.0 + mantissa.astype(jnp.float32) / 8.0) * jnp.where(exponent == 0, 0.25, jnp.where(exponent == 1, 0.5, 1.0))
    signed = (1.0 - 2.0 * sign_bit.astype(jnp.float32)) * magnitude
    return signed.astype(jnp.bfloat16)


def draw_decay_log(key, part):
    key = jax.random.fold_in(key, 23)
    rate_scale = jnp.exp(jax.random.uniform(key, (N_PIPE, HEADS), jnp.float32, jnp.log(3.0), jnp.log(13.0)))
    return jnp.log(rate_scale / BATCH_TOKENS).astype(jnp.float32)


def draw_step_raw(key, part):
    key = jax.random.fold_in(key, 37)
    first_key, following_key = jax.random.split(key)
    baseline_value = jnp.clip(-0.7 + 0.4 * jax.random.normal(first_key, (N_PIPE, BATCH_TOKENS, HEADS), jnp.float32), -2.5, 1.0)
    spike_positions = jax.random.randint(following_key, (N_PIPE, 1, 2), 0, BATCH_TOKENS)
    index_of_token = jnp.arange(BATCH_TOKENS, dtype=jnp.int32)[None, :, None]
    spike_mask = jnp.any(index_of_token == spike_positions, axis=-1)
    return jnp.where(spike_mask[:, :, None], 9.0, baseline_value).astype(jnp.bfloat16)


def plant(drawn, rng, smallest, largest):
    longest = drawn.shape.index(max(drawn.shape))
    spots = []
    for shift in (0, 1):
        where = [jax.random.randint(jax.random.fold_in(rng, axis), (), 0, length) for axis, length in enumerate(drawn.shape)]
        where[longest] = (where[longest] + shift) % drawn.shape[longest]
        spots.append(tuple(where))
    return drawn.at[spots[0]].set(smallest).at[spots[1]].set(largest)


def with_spikes(values, key, source, target, shards_of, factor):
    owner, partner = [(jnp.arange(values.shape[dim]) // (values.shape[dim] // shards_of)).reshape([-1 if axis == dim else 1 for axis in range(values.ndim)]) for dim in (source, target)]
    chosen = jax.random.permutation(key, shards_of)[partner]
    strong = (owner == chosen) | (owner == (partner + shards_of // 2) % shards_of)
    return jnp.where(strong, factor * values, values)


def shard_levels(key, extent, pieces, least, top_value):
    def one(axis_at, blocks):
        heights = jax.random.uniform(jax.random.fold_in(jax.random.fold_in(key, 6), axis_at), (blocks,), jnp.float32, least / len(pieces), top_value / len(pieces))
        return jnp.repeat(jnp.exp(heights), extent[axis_at] // blocks).reshape((-1,) + (1,) * (len(extent) - axis_at - 1))

    factor_of = one(*pieces[0])
    for cut in pieces[1:]:
        factor_of = factor_of * one(*cut)
    return factor_of


def gaussian(key, shape, scale, reach, shards=(), held_as=jnp.bfloat16):
    values = jax.random.normal(key, shape, jnp.float32) * scale
    if len(shards) > 0:
        values = shard_levels(key, shape, shards, -0.22, 0.18) * values
    return jnp.clip(values, min=-reach, max=reach).astype(held_as)


def noise_with(rng, shape, scale, reach, cuts, heavy, kind=jnp.bfloat16):
    array = scale * jax.random.normal(rng, shape, jnp.float32)
    if cuts:
        array = array * shard_levels(rng, shape, cuts, -0.22, 0.18)
    return jnp.clip(with_spikes(array, jax.random.fold_in(rng, 3), *heavy), -reach, reach).astype(kind)


def setup_inputs(seed: int = 0) -> dict:
    keys = jax.random.split(jax.random.key(seed), 15)
    mixed_fwd = noise_with(keys[0], (N_PIPE, BATCH_TOKENS, D_INNER), 1.0, 6.0, ((0, 32), (2, 16)), (2, 1, 16, 2.0))
    resid_fwd = gaussian(keys[1], (N_PIPE, BATCH_TOKENS, D), 1.0, 6.0, ((0, 32), (1, 16)))
    weight_vals = draw_weight_vals(jax.random.fold_in(keys[14], 71), 0)
    weight_exps = plant(jax.random.randint(keys[3], (N_PIPE, D_INNER // SCALE_BLOCK), 117, 122), jax.random.fold_in(keys[3], 1), 117, 121).astype(jnp.int32)
    inner_x = gaussian(keys[4], (N_PIPE, BATCH_TOKENS, D_INNER), 1.0, 6.0, ((0, 32), (2, 16)))
    inner_z = gaussian(keys[5], (N_PIPE, BATCH_TOKENS, D_INNER), 1.0, 6.0, ((0, 32), (2, 16)))
    proj_b = gaussian(keys[6], (N_PIPE, BATCH_TOKENS, GROUPS * STATE), 0.3, 2.0, ((0, 32), (2, 16)))
    proj_c = gaussian(keys[7], (N_PIPE, BATCH_TOKENS, GROUPS * STATE), 0.3, 2.0, ((0, 32), (2, 16)))
    step_raw = draw_step_raw(jax.random.fold_in(keys[14], 71), 0)
    step_bias = jnp.clip(jax.random.uniform(keys[9], (N_PIPE, HEADS), jnp.float32, -0.5, 0.5) * shard_levels(keys[9], (N_PIPE, HEADS), ((0, 32), (1, 16)), -0.4, 0.0), -0.5, 0.5)
    decay_log = draw_decay_log(jax.random.fold_in(keys[14], 71), 0)
    head_skip_weight = jnp.clip(0.5 + 1.0 * jax.random.uniform(keys[11], (N_PIPE, HEADS), jnp.float32) ** shard_levels(keys[11], (N_PIPE, HEADS), ((0, 32), (1, 16)), -0.2, 0.2), 0.5, 1.5)
    norm_gain = jnp.clip(1.0 + 0.15 * jax.random.normal(keys[12], (N_PIPE, D_INNER), jnp.float32), 0.25, 1.75)
    upstream = gaussian(keys[13], (N_PIPE, BATCH_TOKENS, D), 1.0, 6.0, ((0, 32), (1, 16)))
    return dict(mixed_fwd=mixed_fwd, resid_fwd=resid_fwd, weight_vals=weight_vals, weight_exps=weight_exps, inner_x=inner_x, inner_z=inner_z, proj_b=proj_b, proj_c=proj_c, step_raw=step_raw, step_bias=step_bias, decay_log=decay_log, head_skip_weight=head_skip_weight, norm_gain=norm_gain, upstream=upstream)


EPSILON = 1e-05
HIGHEST = lax.Precision.HIGHEST

def block_scale(exponents):
    depth_left = (127 - exponents).astype(jnp.int32)
    factor = jnp.ones(exponents.shape, jnp.float32)
    for position in range(7):
        switched = depth_left // 2 ** position % 2 == 1
        factor = factor * jnp.where(switched, jnp.float32(0.5 ** 2 ** position), jnp.float32(1.0))
    return factor

def dequantize(weight_codes, exponents):
    row_scale = jnp.repeat(block_scale(exponents), SCALE_BLOCK).astype(jnp.bfloat16)
    return weight_codes * row_scale[:, None]

def mixer(inputs, gate_in, proj_b, proj_c, step_raw, step_bias, decay_log, head_skip_weight, norm_gain):
    length = inputs.shape[0]
    head_count = step_bias.shape[0]
    step_size = jax.nn.softplus(step_raw + step_bias[None, :])
    decay_rate = -jnp.exp(decay_log)
    cumulated = jnp.cumsum(step_size * decay_rate[None, :], axis=0)
    per_head = inputs.reshape(length, head_count, -1)
    keys_b = proj_b.reshape(length, GROUPS, -1)
    query_c = proj_c.reshape(length, GROUPS, -1)
    intersection = jnp.einsum('tgs,ugs->gtu', query_c, keys_b, precision=HIGHEST)
    intersection = jnp.repeat(intersection, head_count // GROUPS, axis=0)
    spread_log = cumulated.T[:, :, None] - cumulated.T[:, None, :]
    causal = jnp.tril(jnp.ones((length, length), dtype=bool))[None]
    decay_table = jnp.where(causal, jnp.exp(jnp.where(causal, spread_log, 0.0)), 0.0)
    weights = decay_table * intersection * step_size.T[:, None, :]
    result = jnp.einsum('htu,uhp->thp', weights, per_head, precision=HIGHEST)
    result = result + head_skip_weight[None, :, None] * per_head
    gated_out = result.reshape(length, GROUPS, -1) * jax.nn.silu(gate_in.reshape(length, GROUPS, -1))
    norm_scale = lax.rsqrt(lax.optimization_barrier(jnp.mean(gated_out * gated_out, axis=-1, keepdims=True)) + EPSILON)
    return (gated_out * norm_scale).reshape(length, -1) * norm_gain[None, :]

def reference(mixed_fwd, resid_fwd, weight_vals, weight_exps, inner_x, inner_z, proj_b, proj_c, step_raw, step_bias, decay_log, head_skip_weight, norm_gain, upstream):

    def section_forward(section_args):
        mixed, residual, weight_codes, exponents = section_args
        weight = dequantize(weight_codes, exponents)
        summed = jnp.dot(mixed, weight, preferred_element_type=jnp.float32)
        return (residual.astype(jnp.float32) + summed).astype(jnp.bfloat16)
    produced = lax.map(section_forward, (mixed_fwd, resid_fwd, weight_vals, weight_exps))
    arriving = jnp.concatenate([jnp.zeros_like(produced[:1]), produced[:-1]], axis=0)
    received = jnp.concatenate([upstream[1:], jnp.zeros_like(upstream[:1])], axis=0)

    def section_backward(section_args):
        weight_codes, exponents, incoming, inputs, gate_in, state_b, state_c, raw_steps, bias_steps, decay_logs, skip_terms, gains = section_args
        weight = dequantize(weight_codes, exponents)
        cotangent = lax.dot_general(incoming, weight, (((1,), (1,)), ((), ())), preferred_element_type=jnp.float32)
        primals = (inputs.astype(jnp.float32), gate_in.astype(jnp.float32), state_b.astype(jnp.float32), state_c.astype(jnp.float32), raw_steps.astype(jnp.float32), bias_steps, decay_logs, skip_terms, gains)
        _, pullback = jax.vjp(mixer, *primals)
        gradients = pullback(cotangent)
        return (gradients[0].astype(jnp.bfloat16), gradients[1].astype(jnp.bfloat16), gradients[2].astype(jnp.bfloat16), gradients[3].astype(jnp.bfloat16), gradients[4].astype(jnp.bfloat16), gradients[5], gradients[6], gradients[7], gradients[8])
    outputs = lax.map(section_backward, (weight_vals, weight_exps, received, inner_x, inner_z, proj_b, proj_c, step_raw, step_bias, decay_log, head_skip_weight, norm_gain))
    return (arriving, outputs[0], outputs[1], outputs[2], outputs[3], outputs[4], outputs[5], outputs[6], outputs[7], outputs[8])
```

```python
import jax
import jax.numpy as jnp
from jax import lax
from jax.experimental import pallas as pl
from jax.experimental.pallas import tpu as pltpu
from jax.sharding import PartitionSpec as P

MESH = pl.DeviceIdType.MESH
HIGHEST = lax.Precision.HIGHEST
F32 = jnp.float32
BF16 = jnp.bfloat16

TOKENS = 128
D = 4096
HALF = D // 2
CHANNELS = 512
HEADS = 8
HEAD_DIM = 64
STATE = 128
ROWS = 8
SCALE_BLOCK = 32
Z_RUN = 8
EPSILON = 1e-05
PARTS = 2
WIDTH = HALF // PARTS


def nt(a, b, precision=None):
    return lax.dot_general(
        a, b, (((1,), (1,)), ((), ())), preferred_element_type=F32, precision=precision
    )


def nn(a, b, precision=None):
    return jnp.dot(a, b, preferred_element_type=F32, precision=precision)


def fold(v):
    n = v.shape[1] // 2
    return jnp.concatenate([v[:, :n], v[:, n:]], axis=0)


def block_scale(exponents):
    depth_left = 127 - exponents
    factor = jnp.ones(exponents.shape, F32)
    for position in range(7):
        switched = ((depth_left >> position) & 1) == 1
        factor = factor * jnp.where(switched, F32(0.5 ** 2**position), F32(1.0))
    return factor


def iota(shape, dim):
    return lax.broadcasted_iota(jnp.int32, shape, dim)


def kernel(
    mixed_hbm, resid_hbm, weight_hbm, exps_hbm, x_hbm, z_hbm, b_hbm, c_hbm, raw_hbm,
    bias_hbm, decay_hbm, skip_hbm, gain_hbm, up_hbm,
    arriving_out, gx_out, gz_out, gb_out, gc_out, gstep_out, gbias_out, gdecay_out, gskip_out, ggain_out,
    mixed, resid, weight, exps, x, z, b, c_in, raw, bias, decay, skip, gain, up,
    up_send, gathered, rows_in, scaled, temp, p_send, p_own, s_recv, q_send, y_recv, r_sum, z_send, z_recv, n_send, n_recv,
    pads, ed, w_t, x_stack, g_table, y_val, normed, q_gate, s_gate,
    arriving, gx, gz, gb, gc, gstep, gbias, gdecay, gskip, ggain,
    load_sem, w_sem, out_sem, ag_send, ag_recv, sib_send, sib_recv, ys_send, ys_recv, zs_send, zs_recv, ns_send, ns_recv,
):
    p, t = lax.axis_index("pipe"), lax.axis_index("tp")
    n_pipe = lax.axis_size("pipe")
    z_lo = p % Z_RUN
    y, z_hi, core = t // 4, (t // 2) % 2, t % 2
    after, before = (p + 1) % n_pipe, (p + n_pipe - 1) % n_pipe
    turn_up = jnp.where(z_lo == Z_RUN - 1, 1, 0)
    turn_down = jnp.where(z_lo == 0, 1, 0)
    near = (z_hi + turn_up) % 2
    near_down = (z_hi + turn_down) % 2
    late = z_hi == 1

    def at(yy, zz, cc):
        return yy * 4 + zz * 2 + cc

    sibling = (p, at(y, z_hi, 1 - core))
    y_peer = [(p, at((y + d) % 4, z_hi, core)) for d in range(4)]
    opposite = (p, at(y, 1 - z_hi, core))

    def load(i, src, dst):
        return pltpu.make_async_copy(src, dst, load_sem.at[i])

    loads = {
        name: load(i, src.at[0] if len(src.shape) == 3 else src, dst)
        for i, (name, src, dst) in enumerate(
            (
                ("up", up_hbm, up), ("mixed", mixed_hbm, mixed), ("exps", exps_hbm, exps), ("resid", resid_hbm, resid),
                ("raw", raw_hbm, raw), ("bias", bias_hbm, bias), ("decay", decay_hbm, decay),
                ("b", b_hbm, b), ("c", c_hbm, c_in), ("x", x_hbm, x), ("z", z_hbm, z),
                ("skip", skip_hbm, skip), ("gain", gain_hbm, gain),
            )
        )
    }

    def columns(side, k):
        half = 1 - core if side == 0 else core
        return pl.ds(pl.multiple_of(half * HALF + k * WIDTH, WIDTH), WIDTH)

    def w_load(side, k):
        cols = columns(side, k)
        return pltpu.make_async_copy(weight_hbm.at[0, :, cols], weight.at[:, cols], w_sem.at[side, k])

    for name in ("up", "mixed", "exps", "resid"):
        loads[name].start()
    for k in range(PARTS):
        for side in range(2):
            w_load(side, k).start()
    for name in ("raw", "bias", "decay", "b", "c", "x", "z", "skip", "gain"):
        loads[name].start()

    far_down = 1 - near_down
    partners = [sibling, *y_peer[1:], opposite]
    partners += [(after, at(y, near, core)), (after, at(y, near, 1 - core)), (after, at(y, 1 - near, core))]
    partners += [(before, at(y, near_down, core)), (before, at(y, near_down, 1 - core)), (before, at(y, far_down, core))]
    barrier = pltpu.get_barrier_semaphore()
    for device in partners:
        pl.semaphore_signal(barrier, inc=1, device_id=device, device_id_type=MESH)

    def remote(src, dst, send, recv, device):
        return pltpu.make_async_remote_copy(
            src_ref=src, dst_ref=dst, send_sem=send, recv_sem=recv, device_id=device, device_id_type=MESH
        )

    loads["up"].wait()
    up_send[...] = fold(up[...].astype(F32)).astype(BF16)

    def gather_copy(i):
        device = (before, at(y, near_down if i == 0 else far_down, core))
        return remote(up_send, gathered.at[t], ag_send.at[i], ag_recv.at[t], device)

    def enter():
        pl.semaphore_wait(barrier, len(partners))
        gather_copy(1).start()
        gather_copy(0).start()

    pl.when(late)(enter)

    def slot(i, d, cc):
        return at((y + d) % 4, near if i == 0 else 1 - near, cc)

    def block_copy(i, d, device, send):
        s = slot(i, d, core)
        return remote(gathered.at[s], gathered.at[s], send, ag_recv.at[s], device)

    def y_gather(i, d):
        return block_copy(i, 0, y_peer[d], ag_send.at[2 + i * 3 + d - 1])

    def sib_gather(i, d):
        return block_copy(i, d, sibling, ag_send.at[8 + i * 4 + d])

    def arrived(s):
        remote(gathered.at[s], gathered.at[s], ag_send.at[0], ag_recv.at[s], sibling).wait_recv()

    loads["mixed"].wait()
    loads["exps"].wait()
    loads["resid"].wait()
    expand = jnp.where(iota((16, CHANNELS), 1) // SCALE_BLOCK == iota((16, CHANNELS), 0), 1.0, 0.0).astype(BF16)
    scale = nn(jnp.broadcast_to(block_scale(exps[...]), (8, 16)).astype(BF16), expand)[:1]
    scaled[...] = (mixed[...].astype(F32) * scale).astype(BF16)
    mine = pl.ds(pl.multiple_of(t * ROWS, ROWS), ROWS)

    def sib_copy(k):
        return remote(p_send.at[k], s_recv.at[k], sib_send.at[k], sib_recv.at[k], sibling)

    for k in range(PARTS):
        for side in range(2):
            w_load(side, k).wait()
            target = temp if side == 0 else p_own.at[k]
            cols = columns(side, k)
            target[...] = nn(scaled[...], weight[:, cols])
            target[mine, :] += resid[:, cols].astype(F32)
            if side == 0:
                p_send[k] = temp[...].astype(BF16)
                pl.when(late)(lambda k=k: sib_copy(k).start())

    def mixer_forward():
        for name in ("raw", "bias", "decay", "b", "c", "x", "z", "skip", "gain"):
            loads[name].wait()
        pads[...] = jnp.zeros_like(pads)
        pads[0, :, :HEADS] = raw[...].astype(F32) + bias[...]
        pads[2, :, :HEADS] = jnp.broadcast_to(decay[...], (TOKENS, HEADS))
        stepped = pads[0]
        size = jnp.maximum(stepped, 0.0) + jnp.log1p(jnp.exp(-jnp.abs(stepped)))
        rate = -jnp.exp(pads[2])
        pads[1] = size
        pads[2] = rate
        row, col = iota((TOKENS, TOKENS), 0), iota((TOKENS, TOKENS), 1)
        lower = jnp.where(row >= col, 1.0, 0.0)
        cumulated = nn(lower, size * rate, HIGHEST)
        cumulated_t = cumulated.T
        size_t = size.T
        g_table[...] = nt(c_in[...], b[...])
        table = g_table[...]
        lane = iota((TOKENS, 128), 1)
        head_of = jnp.where(iota((8, CHANNELS), 1) // HEAD_DIM == iota((8, CHANNELS), 0), 1.0, 0.0)
        skip_row = nn(jnp.broadcast_to(skip[...], (8, HEADS)), head_of, HIGHEST)[:1]
        for pair in range(HEADS // 2):
            cols = slice(pair * 128, pair * 128 + 128)
            xp = x[:, cols].astype(F32)
            x_stack[pair, :TOKENS] = jnp.where(lane < HEAD_DIM, xp, 0.0).astype(BF16)
            x_stack[pair, TOKENS:] = jnp.where(lane < HEAD_DIM, 0.0, xp).astype(BF16)
            ws = []
            for j in range(2):
                h = pair * 2 + j
                spread = cumulated[:, h : h + 1] - cumulated_t[h : h + 1, :]
                e = jnp.exp(jnp.where(row >= col, spread, -1e30)) * size_t[h : h + 1, :]
                ed[h] = e
                w = e * table
                w_t[pair, :, j * TOKENS : (j + 1) * TOKENS] = w.T.astype(BF16)
                ws.append(w.astype(BF16))
            y_val[:, cols] = nn(jnp.concatenate(ws, axis=1), x_stack[pair]) + skip_row[:, cols] * xp
        zf = z[...].astype(F32)
        sig = 1.0 / (1.0 + jnp.exp(-zf))
        silu = zf * sig
        gated = y_val[...] * silu
        r = lax.rsqrt(jnp.mean(gated * gated, axis=1, keepdims=True) + EPSILON)
        normed[...] = gated * r
        s_gate[...] = silu * r
        q_gate[...] = y_val[...] * (sig + silu * (1.0 - sig)) * r

    @pl.when(z_hi == 0)
    def _():
        mixer_forward()
        enter()
        for k in range(PARTS):
            sib_copy(k).start()

    def y_copy(k, d):
        to = (y + d) % 4
        return remote(
            q_send.at[k, pl.ds(pl.multiple_of(to * 32, 32), 32)], y_recv.at[k, d - 1],
            ys_send.at[k, d - 1], ys_recv.at[k, d - 1], y_peer[d],
        )

    for k in range(PARTS):
        sib_copy(k).wait()
        total = p_own[k] + s_recv[k].astype(F32)
        p_own[k] = total
        q_send[k] = total.astype(BF16)
        for d in (2, 1, 3):
            y_copy(k, d).start()

    pl.when(late)(mixer_forward)

    for i in range(2):
        arrived(slot(i, 0, core))
        for d in (2, 1, 3):
            y_gather(i, d).start()
        sib_gather(i, 0).start()

    def z_copy(k):
        return remote(z_send.at[k], z_recv.at[k], zs_send.at[k], zs_recv.at[k], opposite)

    keep = pl.ds(pl.multiple_of(near * 16, 16), 16)
    give = pl.ds(pl.multiple_of((1 - near) * 16, 16), 16)
    for k in range(PARTS):
        for d in (1, 2, 3):
            y_copy(k, d).wait()
        total = p_own[k, pl.ds(pl.multiple_of(y * 32, 32), 32), :]
        for d in range(3):
            total += y_recv[k, d].astype(F32)
        r_sum[k] = total
        z_send[k] = r_sum[k, give, :].astype(BF16)
        z_copy(k).start()

    for i in range(2):
        for d in (1, 3, 2):
            arrived(slot(i, d, core))
            sib_gather(i, d).start()

    def n_copy(k, cc):
        return remote(
            n_send.at[k, cc], n_recv.at[k, core], ns_send.at[k, cc], ns_recv.at[k, core], (after, at(y, near, cc))
        )

    for k in range(PARTS):
        z_copy(k).wait()
        total = r_sum[k, keep, :] + z_recv[k].astype(F32)
        for cc in range(2):
            n_send[k, cc] = fold(total[cc * ROWS : (cc + 1) * ROWS]).astype(BF16)
            n_copy(k, cc).start()

    for i in range(2):
        for d in range(4):
            arrived(slot(i, d, 1 - core))
    for m in range(8):
        first, second = gathered[2 * m].astype(F32), gathered[2 * m + 1].astype(F32)
        for j in range(2):
            part = jnp.concatenate([first[j * 8 : j * 8 + 8], second[j * 8 : j * 8 + 8]], axis=0)
            rows_in[m * 16 : m * 16 + 16, j * HALF : (j + 1) * HALF] = part.astype(BF16)
    fed = jnp.where(p == n_pipe - 1, 0.0, 1.0)
    cotangent = nt(rows_in[...], weight[...]) * (scale * fed)

    n_val = normed[...]
    cn = cotangent * n_val
    ggain[...] = jnp.sum(cn, axis=0, keepdims=True)
    inner = jnp.mean(cn * gain[...], axis=1, keepdims=True)
    base = cotangent * gain[...] - n_val * inner
    gz[...] = (base * q_gate[...]).astype(BF16)
    dy = base * s_gate[...]
    head_cols = jnp.where(iota((CHANNELS, 128), 0) // HEAD_DIM == iota((CHANNELS, 128), 1), 1.0, 0.0)
    skip_cols = jnp.sum(dy * x[...].astype(F32), axis=0, keepdims=True)
    gskip[...] = nn(jnp.broadcast_to(skip_cols, (8, CHANNELS)), head_cols, HIGHEST)[:1, :HEADS]
    head_of = jnp.where(iota((8, CHANNELS), 1) // HEAD_DIM == iota((8, CHANNELS), 0), 1.0, 0.0)
    skip_row = nn(jnp.broadcast_to(skip[...], (8, HEADS)), head_of, HIGHEST)[:1]
    table = g_table[...]
    lane = iota((TOKENS, 128), 1)
    sub = iota((128, TOKENS), 0)
    d_table = jnp.zeros((TOKENS, TOKENS), F32)
    row_sums = jnp.zeros((TOKENS, 128), F32)
    col_sums = jnp.zeros((128, TOKENS), F32)
    for pair in range(HEADS // 2):
        cols = slice(pair * 128, pair * 128 + 128)
        dyp = dy[:, cols]
        d_w = nt(dyp.astype(BF16), x_stack[pair])
        stack = jnp.concatenate(
            [jnp.where(lane < HEAD_DIM, dyp, 0.0), jnp.where(lane < HEAD_DIM, 0.0, dyp)], axis=0
        ).astype(BF16)
        gx[:, cols] = (nn(w_t[pair], stack) + skip_row[:, cols] * dyp).astype(BF16)
        for j in range(2):
            h = pair * 2 + j
            t_h = d_w[:, j * TOKENS : (j + 1) * TOKENS] * ed[h]
            d_table += t_h
            s_h = t_h * table
            row_sums = jnp.where(lane == h, jnp.sum(s_h, axis=1, keepdims=True), row_sums)
            col_sums = jnp.where(sub == h, jnp.sum(s_h, axis=0, keepdims=True), col_sums)
    gc[...] = nn(d_table.astype(BF16), b[...]).astype(BF16)
    gb[...] = nn(d_table.T.astype(BF16), c_in[...]).astype(BF16)
    direct = col_sums.T
    row, col = iota((TOKENS, TOKENS), 0), iota((TOKENS, TOKENS), 1)
    upper = jnp.where(col >= row, 1.0, 0.0)
    carried = nn(upper, row_sums - direct, HIGHEST)
    size, rate = pads[1], pads[2]
    d_size = direct / size + rate * carried
    d_step = d_size / (1.0 + jnp.exp(-pads[0]))
    gstep[...] = d_step[:, :HEADS].astype(BF16)
    gbias[...] = jnp.sum(d_step, axis=0, keepdims=True)[:, :HEADS]
    gdecay[...] = jnp.sum(size * rate * carried, axis=0, keepdims=True)[:, :HEADS]

    held = jnp.where(p == 0, 0.0, 1.0)
    for k in range(PARTS):
        for cc in range(2):
            remote(
                n_send.at[k, 0], n_recv.at[k, cc], ns_send.at[k, 0], ns_recv.at[k, cc], sibling
            ).wait_recv()
            got = n_recv[k, cc].astype(F32) * held
            start = cc * HALF + k * WIDTH
            arriving[:, start : start + WIDTH // 2] = got[:8].astype(BF16)
            arriving[:, start + WIDTH // 2 : start + WIDTH] = got[8:].astype(BF16)

    stores = [
        pltpu.make_async_copy(src, dst.at[0] if len(dst.shape) == 3 else dst, out_sem.at[i])
        for i, (src, dst) in enumerate(
            (
                (arriving, arriving_out), (gx, gx_out), (gz, gz_out), (gb, gb_out), (gc, gc_out), (gstep, gstep_out),
                (gbias, gbias_out), (gdecay, gdecay_out), (gskip, gskip_out), (ggain, ggain_out),
            )
        )
    ]
    for store in stores:
        store.start()
    for store in stores:
        store.wait()
    for i in range(2):
        gather_copy(i).wait_send()
        for d in (1, 2, 3):
            y_gather(i, d).wait_send()
        for d in range(4):
            sib_gather(i, d).wait_send()
    for k in range(PARTS):
        for cc in range(2):
            n_copy(k, cc).wait_send()


def solution(mesh):
    in_specs = (
        P("pipe", None, "tp"),
        P("pipe", "tp", None),
        P("pipe", "tp", None),
        P("pipe", "tp"),
        P("pipe", None, "tp"),
        P("pipe", None, "tp"),
        P("pipe", None, "tp"),
        P("pipe", None, "tp"),
        P("pipe", None, "tp"),
        P("pipe", "tp"),
        P("pipe", "tp"),
        P("pipe", "tp"),
        P("pipe", "tp"),
        P("pipe", "tp", None),
    )
    out_specs = (
        P("pipe", "tp", None),
        P("pipe", None, "tp"),
        P("pipe", None, "tp"),
        P("pipe", None, "tp"),
        P("pipe", None, "tp"),
        P("pipe", None, "tp"),
        P("pipe", "tp"),
        P("pipe", "tp"),
        P("pipe", "tp"),
        P("pipe", "tp"),
    )
    out_shape = [
        jax.ShapeDtypeStruct(shape, dtype)
        for shape, dtype in (
            ((1, ROWS, D), BF16),
            ((1, TOKENS, CHANNELS), BF16),
            ((1, TOKENS, CHANNELS), BF16),
            ((1, TOKENS, STATE), BF16),
            ((1, TOKENS, STATE), BF16),
            ((1, TOKENS, HEADS), BF16),
            ((1, HEADS), F32),
            ((1, HEADS), F32),
            ((1, HEADS), F32),
            ((1, CHANNELS), F32),
        )
    ]
    vmem = pltpu.VMEM
    dma = pltpu.SemaphoreType.DMA
    scratch = [
        vmem((TOKENS, CHANNELS), BF16), vmem((ROWS, D), BF16), vmem((CHANNELS, D), BF16), vmem((1, 16), jnp.int32),
        vmem((TOKENS, CHANNELS), BF16), vmem((TOKENS, CHANNELS), BF16), vmem((TOKENS, STATE), BF16),
        vmem((TOKENS, STATE), BF16), vmem((TOKENS, HEADS), BF16), vmem((1, HEADS), F32), vmem((1, HEADS), F32),
        vmem((1, HEADS), F32), vmem((1, CHANNELS), F32), vmem((ROWS, D), BF16),
        vmem((16, HALF), BF16), vmem((16, 16, HALF), BF16), vmem((TOKENS, D), BF16), vmem((TOKENS, CHANNELS), BF16),
        vmem((TOKENS, WIDTH), F32), vmem((PARTS, TOKENS, WIDTH), BF16), vmem((PARTS, TOKENS, WIDTH), F32),
        vmem((PARTS, TOKENS, WIDTH), BF16), vmem((PARTS, TOKENS, WIDTH), BF16), vmem((PARTS, 3, 32, WIDTH), BF16),
        vmem((PARTS, 32, WIDTH), F32), vmem((PARTS, 16, WIDTH), BF16), vmem((PARTS, 16, WIDTH), BF16),
        vmem((PARTS, 2, 16, WIDTH // 2), BF16), vmem((PARTS, 2, 16, WIDTH // 2), BF16),
        vmem((3, TOKENS, 128), F32), vmem((HEADS, TOKENS, TOKENS), F32), vmem((HEADS // 2, TOKENS, 2 * TOKENS), BF16),
        vmem((HEADS // 2, 2 * TOKENS, 128), BF16), vmem((TOKENS, TOKENS), F32), vmem((TOKENS, CHANNELS), F32),
        vmem((TOKENS, CHANNELS), F32), vmem((TOKENS, CHANNELS), F32), vmem((TOKENS, CHANNELS), F32),
        vmem((ROWS, D), BF16), vmem((TOKENS, CHANNELS), BF16), vmem((TOKENS, CHANNELS), BF16),
        vmem((TOKENS, STATE), BF16), vmem((TOKENS, STATE), BF16), vmem((TOKENS, HEADS), BF16), vmem((1, HEADS), F32),
        vmem((1, HEADS), F32), vmem((1, HEADS), F32), vmem((1, CHANNELS), F32),
        dma((13,)), dma((2, PARTS)), dma((10,)), dma((16,)), dma((16,)), dma((PARTS,)), dma((PARTS,)),
        dma((PARTS, 3)), dma((PARTS, 3)), dma((PARTS,)), dma((PARTS,)), dma((PARTS, 2)), dma((PARTS, 2)),
    ]
    any_space = pl.BlockSpec(memory_space=pl.ANY)
    call = pl.pallas_call(
        kernel,
        out_shape=out_shape,
        in_specs=[any_space] * 14,
        out_specs=[any_space] * 10,
        scratch_shapes=scratch,
        compiler_params=pltpu.CompilerParams(
            collective_id=0, has_side_effects=True, vmem_limit_bytes=48 * 1024 * 1024
        ),
        cost_estimate=pl.CostEstimate(flops=1_200_000_000, bytes_accessed=6_000_000, transcendentals=500_000),
    )

    def on_device(*blocks):
        return tuple(call(*blocks))

    return jax.shard_map(on_device, mesh=mesh, in_specs=in_specs, out_specs=out_specs, check_vma=False)
```

```python
import jax
import jax.numpy as jnp
from jax import lax
from jax.experimental import pallas as pl
from jax.experimental.pallas import tpu as pltpu
from jax.sharding import PartitionSpec as P

MESH = pl.DeviceIdType.MESH
HIGHEST = lax.Precision.HIGHEST
F32 = jnp.float32
BF16 = jnp.bfloat16

TOKENS = 128
D = 4096
HALF = D // 2
CHANNELS = 512
HEADS = 8
HEAD_DIM = 64
STATE = 128
ROWS = 8
SCALE_BLOCK = 32
Z_RUN = 8
EPSILON = 1e-05
PARTS = 2
WIDTH = HALF // PARTS


def nt(a, b, precision=None):
    return lax.dot_general(
        a, b, (((1,), (1,)), ((), ())), preferred_element_type=F32, precision=precision
    )


def nn(a, b, precision=None):
    return jnp.dot(a, b, preferred_element_type=F32, precision=precision)


def fold(v):
    n = v.shape[1] // 2
    return jnp.concatenate([v[:, :n], v[:, n:]], axis=0)


def block_scale(exponents):
    depth_left = 127 - exponents
    factor = jnp.ones(exponents.shape, F32)
    for position in range(7):
        switched = ((depth_left >> position) & 1) == 1
        factor = factor * jnp.where(switched, F32(0.5 ** 2**position), F32(1.0))
    return factor


def iota(shape, dim):
    return lax.broadcasted_iota(jnp.int32, shape, dim)


def kernel(
    mixed_hbm, resid_hbm, weight_hbm, exps_hbm, x_hbm, z_hbm, b_hbm, c_hbm, raw_hbm,
    bias_hbm, decay_hbm, skip_hbm, gain_hbm, up_hbm,
    arriving, gx, gz, gb, gc, gstep, gbias, gdecay, gskip, ggain,
    mixed, resid, weight, exps, x, z, b, c_in, raw, bias, decay, skip, gain, up,
    up_send, gathered, rows_in, scaled, temp, p_send, p_own, s_recv, q_send, y_recv, r_sum, z_send, z_recv, n_send, n_recv,
    pads, ed, w_t, x_stack, g_table, y_val, normed, q_gate, s_gate,
    load_sem, w_sem, ready, ag_send, ag_recv, sib_send, sib_recv, ys_send, ys_recv, zs_send, zs_recv, ns_send, ns_recv,
):
    p, t = lax.axis_index("pipe"), lax.axis_index("tp")
    n_pipe = lax.axis_size("pipe")
    z_lo = p % Z_RUN
    y, z_hi, core = t // 4, (t // 2) % 2, t % 2
    after, before = (p + 1) % n_pipe, (p + n_pipe - 1) % n_pipe
    turn_up = jnp.where(z_lo == Z_RUN - 1, 1, 0)
    turn_down = jnp.where(z_lo == 0, 1, 0)
    near = (z_hi + turn_up) % 2
    near_down = (z_hi + turn_down) % 2
    late = z_hi == 1

    def at(yy, zz, cc):
        return yy * 4 + zz * 2 + cc

    sibling = (p, at(y, z_hi, 1 - core))
    y_peer = [(p, at((y + d) % 4, z_hi, core)) for d in range(4)]
    opposite = (p, at(y, 1 - z_hi, core))

    def load(i, src, dst):
        return pltpu.make_async_copy(src, dst, load_sem.at[i])

    loads = {
        name: load(i, src.at[0] if len(src.shape) == 3 else src, dst)
        for i, (name, src, dst) in enumerate(
            (
                ("up", up_hbm, up), ("mixed", mixed_hbm, mixed), ("exps", exps_hbm, exps), ("resid", resid_hbm, resid),
                ("raw", raw_hbm, raw), ("bias", bias_hbm, bias), ("decay", decay_hbm, decay),
                ("b", b_hbm, b), ("c", c_hbm, c_in), ("x", x_hbm, x), ("z", z_hbm, z),
                ("skip", skip_hbm, skip), ("gain", gain_hbm, gain),
            )
        )
    }

    def columns(side, k):
        half = 1 - core if side == 0 else core
        return pl.ds(pl.multiple_of(half * HALF + k * WIDTH, WIDTH), WIDTH)

    def w_load(side, k):
        cols = columns(side, k)
        return pltpu.make_async_copy(weight_hbm.at[0, :, cols], weight.at[:, cols], w_sem.at[side, k])

    for name in ("up", "mixed", "exps", "resid"):
        loads[name].start()
    for k in range(PARTS):
        for side in range(2):
            w_load(side, k).start()
    for name in ("raw", "bias", "decay", "b", "c", "x", "z", "skip", "gain"):
        loads[name].start()

    def flag(condition):
        return jnp.where(condition, 1, 0)

    far_down = 1 - near_down
    odd = z_lo % 2
    first = flag(z_hi == 0)
    at_start = first * turn_down
    at_half = first * turn_up
    from_half = (1 - first) * turn_down
    from_end = (1 - first) * turn_up
    sends_far = odd + at_start
    gets_far = (1 - odd) + at_half
    forwards = odd * (1 - from_end)
    partners = [(device, 1, 0, 1, 0, 0) for device in (sibling, *y_peer[1:])]
    partners += [
        (opposite, 1, first, 1, 1 - first, 1),
        ((after, at(y, near, core)), 1, at_half, 1, from_end, 0),
        ((after, at(y, near, 1 - core)), 1, at_half, 0, 0, 0),
        ((after, at(y, 1 - near, core)), 0, 0, gets_far, near, 1),
        ((before, at(y, near_down, core)), 1, at_start, 1, from_half, 0),
        ((before, at(y, near_down, 1 - core)), 0, 0, 1, from_half, 0),
        ((before, at(y, far_down, core)), sends_far, first, 0, 0, 1),
    ]
    barrier = pltpu.get_barrier_semaphore()

    def tell(semaphore, device):
        pl.semaphore_signal(semaphore, inc=1, device_id=device, device_id_type=MESH)

    greeted, readied = 0, [0, 0]
    for device, to_it, to_held, from_it, from_held, which in partners:
        greet = from_it * (1 - from_held) + to_it * to_held
        pl.when(greet > 0)(lambda device=device: tell(barrier, device))
        greeted += flag(to_it * (1 - to_held) + from_it * from_held > 0)
        readied[which] += to_it * to_held

    def remote(src, dst, send, recv, device):
        return pltpu.make_async_remote_copy(
            src_ref=src, dst_ref=dst, send_sem=send, recv_sem=recv, device_id=device, device_id_type=MESH
        )

    loads["up"].wait()
    up_send[...] = fold(up[...].astype(F32)).astype(BF16)

    def gather_copy(i):
        device = (before, at(y, near_down if i == 0 else far_down, core))
        return remote(up_send, gathered.at[t], ag_send.at[i], ag_recv.at[t], device)

    def enter():
        pl.semaphore_wait(barrier, greeted)
        pl.when(sends_far * z_hi == 1)(gather_copy(1).start)
        pl.when(at_start == 0)(gather_copy(0).start)
        for device, _, _, from_it, from_held, which in partners:
            pl.when(from_it * from_held == 1)(lambda device=device, which=which: tell(ready.at[which], device))

    pl.when(late)(enter)

    def slot(i, d, cc):
        return at((y + d) % 4, near if i == 0 else 1 - near, cc)

    def block_copy(i, d, device, send):
        s = slot(i, d, core)
        return remote(gathered.at[s], gathered.at[s], send, ag_recv.at[s], device)

    def y_gather(i, d):
        return block_copy(i, 0, y_peer[d], ag_send.at[2 + i * 3 + d - 1])

    def sib_gather(i, d):
        return block_copy(i, d, sibling, ag_send.at[8 + i * 4 + d])

    def arrived(s):
        remote(gathered.at[s], gathered.at[s], ag_send.at[0], ag_recv.at[s], sibling).wait_recv()

    loads["mixed"].wait()
    loads["exps"].wait()
    loads["resid"].wait()
    expand = jnp.where(iota((16, CHANNELS), 1) // SCALE_BLOCK == iota((16, CHANNELS), 0), 1.0, 0.0).astype(BF16)
    scale = nn(jnp.broadcast_to(block_scale(exps[...]), (8, 16)).astype(BF16), expand)[:1]
    for part in range(2):
        for yy in range(4):
            rows = pl.ds(pl.multiple_of(yy * 32 + (1 - near if part == 0 else near) * 16, 16), 16)
            scaled[part * 64 + yy * 16 : part * 64 + yy * 16 + 16] = (mixed[rows].astype(F32) * scale).astype(BF16)
    mine = pl.ds(pl.multiple_of((1 - turn_up) * 64 + y * 16 + core * ROWS, ROWS), ROWS)

    def sib_copy(part, k):
        rows = pl.ds(part * 64, 64)
        return remote(p_send.at[k, rows], s_recv.at[k, rows], sib_send.at[part, k], sib_recv.at[part, k], sibling)

    for k in range(PARTS):
        for side in range(2):
            w_load(side, k).wait()
            target = temp if side == 0 else p_own.at[k]
            cols = columns(side, k)
            target[...] = nn(scaled[...], weight[:, cols])
            target[mine, :] += resid[:, cols].astype(F32)
            if side == 0:
                p_send[k] = temp[...].astype(BF16)
                for part in range(2):
                    pl.when(late)(sib_copy(part, k).start)

    def forward_copy():
        return block_copy(0, 0, opposite, ag_send.at[16])

    @pl.when(late)
    def _():
        arrived(slot(0, 0, core))
        pl.when(forwards == 1)(forward_copy().start)

    @pl.when(z_hi == 0)
    def _():
        enter()
        for part in range(2):
            for k in range(PARTS):
                sib_copy(part, k).start()

    def y_copy(part, k, d):
        to = (y + d) % 4
        return remote(
            q_send.at[k, pl.ds(pl.multiple_of(part * 64 + to * 16, 16), 16)], y_recv.at[part, k, d - 1],
            ys_send.at[part, k, d - 1], ys_recv.at[part, k, d - 1], y_peer[d],
        )

    def pair_sum(part):
        rows = slice(part * 64, part * 64 + 64)
        for k in range(PARTS):
            sib_copy(part, k).wait()
            total = p_own[k, rows] + s_recv[k, rows].astype(F32)
            p_own[k, rows] = total
            q_send[k, rows] = total.astype(BF16)
            for d in (2, 1, 3):
                y_copy(part, k, d).start()

    def section_sum(part, k):
        for d in (1, 2, 3):
            y_copy(part, k, d).wait()
        total = p_own[k, pl.ds(pl.multiple_of(part * 64 + y * 16, 16), 16), :]
        for d in range(3):
            total += y_recv[part, k, d].astype(F32)
        return total

    def z_copy(k):
        return remote(z_send.at[k], z_recv.at[k], zs_send.at[k], zs_recv.at[k], opposite)

    pair_sum(0)

    def mixer_forward():
        for name in ("raw", "bias", "decay", "b", "c", "x", "z", "skip", "gain"):
            loads[name].wait()
        pads[...] = jnp.zeros_like(pads)
        pads[1, :HEADS, :] = raw[...].astype(F32)
        pads[0] = pads[1].T
        pads[0, :, :HEADS] += bias[...]
        pads[2, :, :HEADS] = jnp.broadcast_to(decay[...], (TOKENS, HEADS))
        stepped = pads[0]
        size = jnp.maximum(stepped, 0.0) + jnp.log1p(jnp.exp(-jnp.abs(stepped)))
        rate = -jnp.exp(pads[2])
        pads[1] = size
        pads[2] = rate
        row, col = iota((TOKENS, TOKENS), 0), iota((TOKENS, TOKENS), 1)
        lower = jnp.where(row >= col, 1.0, 0.0)
        cumulated = nn(lower, size * rate, HIGHEST)
        cumulated_t = cumulated.T
        size_t = size.T
        g_table[...] = nt(c_in[...], b[...])
        table = g_table[...]
        lane = iota((TOKENS, 128), 1)
        head_of = jnp.where(iota((8, CHANNELS), 1) // HEAD_DIM == iota((8, CHANNELS), 0), 1.0, 0.0)
        skip_row = nn(jnp.broadcast_to(skip[...], (8, HEADS)), head_of, HIGHEST)[:1]
        for pair in range(HEADS // 2):
            cols = slice(pair * 128, pair * 128 + 128)
            xp = x[:, cols].astype(F32)
            x_stack[pair, :TOKENS] = jnp.where(lane < HEAD_DIM, xp, 0.0).astype(BF16)
            x_stack[pair, TOKENS:] = jnp.where(lane < HEAD_DIM, 0.0, xp).astype(BF16)
            ws = []
            for j in range(2):
                h = pair * 2 + j
                spread = cumulated[:, h : h + 1] - cumulated_t[h : h + 1, :]
                e = jnp.exp(jnp.where(row >= col, spread, -1e30)) * size_t[h : h + 1, :]
                ed[h] = e
                w = e * table
                w_t[pair, :, j * TOKENS : (j + 1) * TOKENS] = w.T.astype(BF16)
                ws.append(w.astype(BF16))
            y_val[:, cols] = nn(jnp.concatenate(ws, axis=1), x_stack[pair]) + skip_row[:, cols] * xp
        zf = z[...].astype(F32)
        sig = 1.0 / (1.0 + jnp.exp(-zf))
        silu = zf * sig
        gated = y_val[...] * silu
        r = lax.rsqrt(jnp.mean(gated * gated, axis=1, keepdims=True) + EPSILON)
        normed[...] = gated * r
        s_gate[...] = silu * r
        q_gate[...] = y_val[...] * (sig + silu * (1.0 - sig)) * r

    mixer_forward()

    for k in range(PARTS):
        z_send[k] = section_sum(0, k).astype(BF16)
        pl.when(late)(z_copy(k).start)
    pair_sum(1)

    def hand_on(i):
        for d in (2, 1, 3):
            y_gather(i, d).start()
        sib_gather(i, 0).start()

    def hand_over(i):
        for d in (1, 3, 2):
            arrived(slot(i, d, core))
            sib_gather(i, d).start()

    @pl.when(z_hi == 0)
    def _():
        pl.when(readied[0] > 0)(lambda: pl.semaphore_wait(ready.at[0], readied[0]))
        pl.when(at_start == 1)(gather_copy(0).start)
        arrived(slot(0, 0, core))

    hand_on(0)

    @pl.when(z_hi == 0)
    def _():
        pl.semaphore_wait(ready.at[1], readied[1])
        for k in range(PARTS):
            z_copy(k).start()
        pl.when(sends_far == 1)(gather_copy(1).start)
        pl.when(forwards == 1)(forward_copy().start)

    for k in range(PARTS):
        r_sum[k] = section_sum(1, k)
    hand_over(0)
    def n_copy(k, cc):
        return remote(
            n_send.at[k, cc], n_recv.at[k, core], ns_send.at[k, cc], ns_recv.at[k, core], (after, at(y, near, cc))
        )

    def produce():
        for k in range(PARTS):
            z_copy(k).wait()
            total = r_sum[k] + z_recv[k].astype(F32)
            for cc in range(2):
                n_send[k, cc] = fold(total[cc * ROWS : (cc + 1) * ROWS]).astype(BF16)
                n_copy(k, cc).start()

    pl.when(late)(produce)
    arrived(slot(1, 0, core))
    hand_on(1)
    hand_over(1)
    pl.when(z_hi == 0)(produce)

    for i in range(2):
        for d in range(4):
            arrived(slot(i, d, 1 - core))
    for m in range(8):
        first, second = gathered[2 * m].astype(F32), gathered[2 * m + 1].astype(F32)
        for j in range(2):
            part = jnp.concatenate([first[j * 8 : j * 8 + 8], second[j * 8 : j * 8 + 8]], axis=0)
            rows_in[m * 16 : m * 16 + 16, j * HALF : (j + 1) * HALF] = part.astype(BF16)
    fed = jnp.where(p == n_pipe - 1, 0.0, 1.0)
    cotangent = nt(rows_in[...], weight[...]) * (scale * fed)

    n_val = normed[...]
    cn = cotangent * n_val
    ggain[...] = jnp.sum(cn, axis=0, keepdims=True)
    inner = jnp.mean(cn * gain[...], axis=1, keepdims=True)
    base = cotangent * gain[...] - n_val * inner
    gz[0] = (base * q_gate[...]).astype(BF16)
    dy = base * s_gate[...]
    head_cols = jnp.where(iota((CHANNELS, 128), 0) // HEAD_DIM == iota((CHANNELS, 128), 1), 1.0, 0.0)
    skip_cols = jnp.sum(dy * x[...].astype(F32), axis=0, keepdims=True)
    gskip[...] = nn(jnp.broadcast_to(skip_cols, (8, CHANNELS)), head_cols, HIGHEST)[:1, :HEADS]
    head_of = jnp.where(iota((8, CHANNELS), 1) // HEAD_DIM == iota((8, CHANNELS), 0), 1.0, 0.0)
    skip_row = nn(jnp.broadcast_to(skip[...], (8, HEADS)), head_of, HIGHEST)[:1]
    table = g_table[...]
    lane = iota((TOKENS, 128), 1)
    sub = iota((128, TOKENS), 0)
    d_table = jnp.zeros((TOKENS, TOKENS), F32)
    row_sums = jnp.zeros((TOKENS, 128), F32)
    col_sums = jnp.zeros((128, TOKENS), F32)
    for pair in range(HEADS // 2):
        cols = slice(pair * 128, pair * 128 + 128)
        dyp = dy[:, cols]
        d_w = nt(dyp.astype(BF16), x_stack[pair])
        stack = jnp.concatenate(
            [jnp.where(lane < HEAD_DIM, dyp, 0.0), jnp.where(lane < HEAD_DIM, 0.0, dyp)], axis=0
        ).astype(BF16)
        gx[0, :, cols] = (nn(w_t[pair], stack) + skip_row[:, cols] * dyp).astype(BF16)
        for j in range(2):
            h = pair * 2 + j
            t_h = d_w[:, j * TOKENS : (j + 1) * TOKENS] * ed[h]
            d_table += t_h
            s_h = t_h * table
            row_sums = jnp.where(lane == h, jnp.sum(s_h, axis=1, keepdims=True), row_sums)
            col_sums = jnp.where(sub == h, jnp.sum(s_h, axis=0, keepdims=True), col_sums)
    gc[0] = nn(d_table.astype(BF16), b[...]).astype(BF16)
    gb[0] = nn(d_table.T.astype(BF16), c_in[...]).astype(BF16)
    direct = col_sums.T
    row, col = iota((TOKENS, TOKENS), 0), iota((TOKENS, TOKENS), 1)
    upper = jnp.where(col >= row, 1.0, 0.0)
    carried = nn(upper, row_sums - direct, HIGHEST)
    size, rate = pads[1], pads[2]
    d_size = direct / size + rate * carried
    d_step = d_size / (1.0 + jnp.exp(-pads[0]))
    gstep[0] = d_step.T[:HEADS].astype(BF16)
    gbias[...] = jnp.sum(d_step, axis=0, keepdims=True)[:, :HEADS]
    gdecay[...] = jnp.sum(size * rate * carried, axis=0, keepdims=True)[:, :HEADS]

    held = jnp.where(p == 0, 0.0, 1.0)
    for k in range(PARTS):
        for cc in range(2):
            remote(
                n_send.at[k, 0], n_recv.at[k, cc], ns_send.at[k, 0], ns_recv.at[k, cc], sibling
            ).wait_recv()
            got = n_recv[k, cc].astype(F32) * held
            start = cc * HALF + k * WIDTH
            arriving[0, :, start : start + WIDTH // 2] = got[:8].astype(BF16)
            arriving[0, :, start + WIDTH // 2 : start + WIDTH] = got[8:].astype(BF16)

    gather_copy(0).wait_send()
    pl.when(sends_far == 1)(gather_copy(1).wait_send)
    pl.when(forwards == 1)(forward_copy().wait_send)
    for i in range(2):
        for d in (1, 2, 3):
            y_gather(i, d).wait_send()
        for d in range(4):
            sib_gather(i, d).wait_send()
    for k in range(PARTS):
        for cc in range(2):
            n_copy(k, cc).wait_send()


def store_all(*refs):
    sem = refs[-1]
    copies = [pltpu.make_async_copy(refs[i], refs[10 + i], sem.at[i]) for i in range(10)]
    for copy in copies:
        copy.start()
    for copy in copies:
        copy.wait()


def solution(mesh):
    in_specs = (
        P("pipe", None, "tp"),
        P("pipe", "tp", None),
        P("pipe", "tp", None),
        P("pipe", "tp"),
        P("pipe", None, "tp"),
        P("pipe", None, "tp"),
        P("pipe", None, "tp"),
        P("pipe", None, "tp"),
        P("pipe", None, "tp"),
        P("pipe", "tp"),
        P("pipe", "tp"),
        P("pipe", "tp"),
        P("pipe", "tp"),
        P("pipe", "tp", None),
    )
    out_specs = (
        P("pipe", "tp", None),
        P("pipe", None, "tp"),
        P("pipe", None, "tp"),
        P("pipe", None, "tp"),
        P("pipe", None, "tp"),
        P("pipe", None, "tp"),
        P("pipe", "tp"),
        P("pipe", "tp"),
        P("pipe", "tp"),
        P("pipe", "tp"),
    )
    out_shape = [
        jax.ShapeDtypeStruct(shape, dtype)
        for shape, dtype in (
            ((1, ROWS, D), BF16),
            ((1, TOKENS, CHANNELS), BF16),
            ((1, TOKENS, CHANNELS), BF16),
            ((1, TOKENS, STATE), BF16),
            ((1, TOKENS, STATE), BF16),
            ((1, HEADS, TOKENS), BF16),
            ((1, HEADS), F32),
            ((1, HEADS), F32),
            ((1, HEADS), F32),
            ((1, CHANNELS), F32),
        )
    ]
    vmem = pltpu.VMEM
    dma = pltpu.SemaphoreType.DMA
    scratch = [
        vmem((TOKENS, CHANNELS), BF16), vmem((ROWS, D), BF16), vmem((CHANNELS, D), BF16), vmem((1, 16), jnp.int32),
        vmem((TOKENS, CHANNELS), BF16), vmem((TOKENS, CHANNELS), BF16), vmem((TOKENS, STATE), BF16),
        vmem((TOKENS, STATE), BF16), vmem((HEADS, TOKENS), BF16), vmem((1, HEADS), F32), vmem((1, HEADS), F32),
        vmem((1, HEADS), F32), vmem((1, CHANNELS), F32), vmem((ROWS, D), BF16),
        vmem((16, HALF), BF16), vmem((16, 16, HALF), BF16), vmem((TOKENS, D), BF16), vmem((TOKENS, CHANNELS), BF16),
        vmem((TOKENS, WIDTH), F32), vmem((PARTS, TOKENS, WIDTH), BF16), vmem((PARTS, TOKENS, WIDTH), F32),
        vmem((PARTS, TOKENS, WIDTH), BF16), vmem((PARTS, TOKENS, WIDTH), BF16), vmem((2, PARTS, 3, 16, WIDTH), BF16),
        vmem((PARTS, 16, WIDTH), F32), vmem((PARTS, 16, WIDTH), BF16), vmem((PARTS, 16, WIDTH), BF16),
        vmem((PARTS, 2, 16, WIDTH // 2), BF16), vmem((PARTS, 2, 16, WIDTH // 2), BF16),
        vmem((3, TOKENS, 128), F32), vmem((HEADS, TOKENS, TOKENS), F32), vmem((HEADS // 2, TOKENS, 2 * TOKENS), BF16),
        vmem((HEADS // 2, 2 * TOKENS, 128), BF16), vmem((TOKENS, TOKENS), F32), vmem((TOKENS, CHANNELS), F32),
        vmem((TOKENS, CHANNELS), F32), vmem((TOKENS, CHANNELS), F32), vmem((TOKENS, CHANNELS), F32),
        dma((13,)), dma((2, PARTS)), pltpu.SemaphoreType.REGULAR((2,)), dma((17,)), dma((16,)), dma((2, PARTS)), dma((2, PARTS)),
        dma((2, PARTS, 3)), dma((2, PARTS, 3)), dma((PARTS,)), dma((PARTS,)), dma((PARTS, 2)), dma((PARTS, 2)),
    ]
    in_hbm = pl.BlockSpec(memory_space=pltpu.HBM)
    in_vmem = pl.BlockSpec(memory_space=pltpu.VMEM)
    call = pl.pallas_call(
        kernel,
        out_shape=[pltpu.VMEM(out.shape, out.dtype) for out in out_shape],
        in_specs=[in_hbm] * 14,
        out_specs=[in_vmem] * 10,
        scratch_shapes=scratch,
        compiler_params=pltpu.CompilerParams(
            collective_id=0, has_side_effects=True, vmem_limit_bytes=48 * 1024 * 1024
        ),
        cost_estimate=pl.CostEstimate(flops=1_200_000_000, bytes_accessed=6_000_000, transcendentals=500_000),
    )

    hand_out = pl.pallas_call(
        store_all,
        out_shape=out_shape,
        in_specs=[in_vmem] * 10,
        out_specs=[in_hbm] * 10,
        scratch_shapes=[dma((10,))],
        cost_estimate=pl.CostEstimate(flops=0, bytes_accessed=900_000, transcendentals=0),
    )

    def on_device(*blocks):
        blocks = list(blocks)
        blocks[8] = jnp.swapaxes(blocks[8], 1, 2)
        blocks = [pltpu.with_memory_space_constraint(block, pltpu.HBM) for block in blocks]
        held = [pltpu.with_memory_space_constraint(result, pltpu.VMEM) for result in call(*blocks)]
        results = list(hand_out(*held))
        results[5] = jnp.swapaxes(results[5], 1, 2)
        return tuple(results)

    return jax.shard_map(on_device, mesh=mesh, in_specs=in_specs, out_specs=out_specs, check_vma=False)
```

```python
import jax
import jax.numpy as jnp
from jax import lax
from jax.experimental import pallas as pl
from jax.experimental.pallas import tpu as pltpu
from jax.sharding import PartitionSpec as P

MESH = pl.DeviceIdType.MESH
HIGHEST = lax.Precision.HIGHEST
F32 = jnp.float32
BF16 = jnp.bfloat16

TOKENS = 128
D = 4096
HALF = D // 2
CHANNELS = 512
HEADS = 8
HEAD_DIM = 64
STATE = 128
ROWS = 8
SCALE_BLOCK = 32
Z_RUN = 8
EPSILON = 1e-05
PARTS = 2
WIDTH = HALF // PARTS


def nt(a, b, precision=None):
    return lax.dot_general(
        a, b, (((1,), (1,)), ((), ())), preferred_element_type=F32, precision=precision
    )


def nn(a, b, precision=None):
    return jnp.dot(a, b, preferred_element_type=F32, precision=precision)


def fold(v):
    n = v.shape[1] // 2
    return jnp.concatenate([v[:, :n], v[:, n:]], axis=0)


def block_scale(exponents):
    depth_left = 127 - exponents
    factor = jnp.ones(exponents.shape, F32)
    for position in range(7):
        switched = ((depth_left >> position) & 1) == 1
        factor = factor * jnp.where(switched, F32(0.5 ** 2**position), F32(1.0))
    return factor


def iota(shape, dim):
    return lax.broadcasted_iota(jnp.int32, shape, dim)


def kernel(
    mixed_hbm, resid_hbm, weight_hbm, exps_hbm, x_hbm, z_hbm, b_hbm, c_hbm, raw_hbm,
    bias_hbm, decay_hbm, skip_hbm, gain_hbm, up_hbm,
    arriving, gx, gz, gb, gc, gstep, gbias, gdecay, gskip, ggain,
    mixed, resid, weight, exps, x, z, b, c_in, raw, bias, decay, skip, gain, up,
    up_send, gathered, rows_in, scaled, temp, p_send, p_own, s_recv, q_send, y_recv, r_sum, z_send, z_recv, n_send, n_recv, f_send, f_recv,
    pads, ed, w_t, x_stack, g_table, y_val, normed, q_gate, s_gate,
    load_sem, w_sem, ready, ag_send, ag_recv, sib_send, sib_recv, ys_send, ys_recv, zs_send, zs_recv, ns_send, ns_recv, fs_send, fs_recv,
):
    p, t = lax.axis_index("pipe"), lax.axis_index("tp")
    n_pipe = lax.axis_size("pipe")
    z_lo = p % Z_RUN
    y, z_hi, core = t // 4, (t // 2) % 2, t % 2
    after, before = (p + 1) % n_pipe, (p + n_pipe - 1) % n_pipe
    turn_up = jnp.where(z_lo == Z_RUN - 1, 1, 0)
    turn_down = jnp.where(z_lo == 0, 1, 0)
    near = (z_hi + turn_up) % 2
    near_down = (z_hi + turn_down) % 2
    late = z_hi == 1

    def at(yy, zz, cc):
        return yy * 4 + zz * 2 + cc

    sibling = (p, at(y, z_hi, 1 - core))
    y_peer = [(p, at((y + d) % 4, z_hi, core)) for d in range(4)]
    opposite = (p, at(y, 1 - z_hi, core))

    def load(i, src, dst):
        return pltpu.make_async_copy(src, dst, load_sem.at[i])

    loads = {
        name: load(i, src.at[0] if len(src.shape) == 3 else src, dst)
        for i, (name, src, dst) in enumerate(
            (
                ("up", up_hbm, up), ("mixed", mixed_hbm, mixed), ("exps", exps_hbm, exps), ("resid", resid_hbm, resid),
                ("raw", raw_hbm, raw), ("bias", bias_hbm, bias), ("decay", decay_hbm, decay),
                ("b", b_hbm, b), ("c", c_hbm, c_in), ("x", x_hbm, x), ("z", z_hbm, z),
                ("skip", skip_hbm, skip), ("gain", gain_hbm, gain),
            )
        )
    }

    def columns(side, k):
        half = 1 - core if side == 0 else core
        return pl.ds(pl.multiple_of(half * HALF + k * WIDTH, WIDTH), WIDTH)

    def w_load(side, k):
        cols = columns(side, k)
        return pltpu.make_async_copy(weight_hbm.at[0, :, cols], weight.at[:, cols], w_sem.at[side, k])

    for name in ("up", "mixed", "exps", "resid"):
        loads[name].start()
    for k in range(PARTS):
        for side in range(2):
            w_load(side, k).start()
    for name in ("raw", "bias", "decay", "b", "c", "x", "z", "skip", "gain"):
        loads[name].start()

    def flag(condition):
        return jnp.where(condition, 1, 0)

    far_down = 1 - near_down
    odd = z_lo % 2
    first = flag(z_hi == 0)
    at_start = first * turn_down
    at_half = first * turn_up
    from_half = (1 - first) * turn_down
    from_end = (1 - first) * turn_up
    sends_far = odd + at_start
    gets_far = (1 - odd) + at_half
    forwards = odd * (1 - from_end)
    swaps_out = 1 - forwards
    swaps_in = (1 - odd) + at_half
    gets_sum = (1 - odd) * (1 - from_half)
    partners = [(device, 1, 0, 1, 0, 0) for device in (sibling, *y_peer[1:])]
    partners += [
        (opposite, 1, first, 1, 1 - first, 1),
        ((after, at(y, near, core)), 1, at_half, 1, from_end, 0),
        ((after, at(y, near, 1 - core)), 1, at_half, 0, 0, 0),
        ((after, at(y, 1 - near, core)), forwards, first * (1 - near), gets_far, near, 1),
        ((after, at(y, 1 - near, 1 - core)), forwards, first * (1 - near), 0, 0, 1),
        ((before, at(y, near_down, core)), 1, at_start, 1, from_half, 0),
        ((before, at(y, near_down, 1 - core)), 0, 0, 1, from_half, 0),
        ((before, at(y, far_down, core)), sends_far, first, gets_sum, (1 - first) * (1 - far_down), 1),
        ((before, at(y, far_down, 1 - core)), 0, 0, gets_sum, (1 - first) * (1 - far_down), 1),
    ]
    barrier = pltpu.get_barrier_semaphore()

    def tell(semaphore, device):
        pl.semaphore_signal(semaphore, inc=1, device_id=device, device_id_type=MESH)

    greeted, readied = 0, [0, 0]
    for device, to_it, to_held, from_it, from_held, which in partners:
        greet = from_it * (1 - from_held) + to_it * to_held
        pl.when(greet > 0)(lambda device=device: tell(barrier, device))
        greeted += flag(to_it * (1 - to_held) + from_it * from_held > 0)
        readied[which] += to_it * to_held

    def remote(src, dst, send, recv, device):
        return pltpu.make_async_remote_copy(
            src_ref=src, dst_ref=dst, send_sem=send, recv_sem=recv, device_id=device, device_id_type=MESH
        )

    loads["up"].wait()
    up_send[...] = fold(up[...].astype(F32)).astype(BF16)

    def gather_copy(i):
        device = (before, at(y, near_down if i == 0 else far_down, core))
        return remote(up_send, gathered.at[t], ag_send.at[i], ag_recv.at[t], device)

    def enter():
        pl.semaphore_wait(barrier, greeted)
        pl.when(sends_far * z_hi == 1)(gather_copy(1).start)
        pl.when(at_start == 0)(gather_copy(0).start)
        for device, _, _, from_it, from_held, which in partners:
            pl.when(from_it * from_held == 1)(lambda device=device, which=which: tell(ready.at[which], device))

    pl.when(late)(enter)

    def slot(i, d, cc):
        return at((y + d) % 4, near if i == 0 else 1 - near, cc)

    def block_copy(i, d, device, send):
        s = slot(i, d, core)
        return remote(gathered.at[s], gathered.at[s], send, ag_recv.at[s], device)

    def y_gather(i, d):
        return block_copy(i, 0, y_peer[d], ag_send.at[2 + i * 3 + d - 1])

    def sib_gather(i, d):
        return block_copy(i, d, sibling, ag_send.at[8 + i * 4 + d])

    def arrived(s):
        remote(gathered.at[s], gathered.at[s], ag_send.at[0], ag_recv.at[s], sibling).wait_recv()

    loads["mixed"].wait()
    loads["exps"].wait()
    loads["resid"].wait()
    expand = jnp.where(iota((16, CHANNELS), 1) // SCALE_BLOCK == iota((16, CHANNELS), 0), 1.0, 0.0).astype(BF16)
    scale = nn(jnp.broadcast_to(block_scale(exps[...]), (8, 16)).astype(BF16), expand)[:1]
    for part in range(2):
        for yy in range(4):
            rows = pl.ds(pl.multiple_of(yy * 32 + (1 - near if part == 0 else near) * 16, 16), 16)
            scaled[part * 64 + yy * 16 : part * 64 + yy * 16 + 16] = (mixed[rows].astype(F32) * scale).astype(BF16)
    mine = pl.ds(pl.multiple_of((1 - turn_up) * 64 + y * 16 + core * ROWS, ROWS), ROWS)

    def sib_copy(part, k):
        rows = pl.ds(part * 64, 64)
        return remote(p_send.at[k, rows], s_recv.at[k, rows], sib_send.at[part, k], sib_recv.at[part, k], sibling)

    for k in range(PARTS):
        for side in range(2):
            w_load(side, k).wait()
            target = temp if side == 0 else p_own.at[k]
            cols = columns(side, k)
            target[...] = nn(scaled[...], weight[:, cols])
            target[mine, :] += resid[:, cols].astype(F32)
            if side == 0:
                p_send[k] = temp[...].astype(BF16)
                for part in range(2):
                    pl.when(late)(sib_copy(part, k).start)

    def forward_copy():
        return block_copy(0, 0, opposite, ag_send.at[16])

    @pl.when((1 - first) * (1 - from_end) == 1)
    def _():
        arrived(slot(0, 0, core))
        pl.when(forwards == 1)(forward_copy().start)

    @pl.when(z_hi == 0)
    def _():
        enter()
        for part in range(2):
            for k in range(PARTS):
                sib_copy(part, k).start()

    def y_copy(part, k, d):
        to = (y + d) % 4
        return remote(
            q_send.at[k, pl.ds(pl.multiple_of(part * 64 + to * 16, 16), 16)], y_recv.at[part, k, d - 1],
            ys_send.at[part, k, d - 1], ys_recv.at[part, k, d - 1], y_peer[d],
        )

    def pair_sum(part):
        rows = slice(part * 64, part * 64 + 64)
        for k in range(PARTS):
            sib_copy(part, k).wait()
            total = p_own[k, rows] + s_recv[k, rows].astype(F32)
            p_own[k, rows] = total
            q_send[k, rows] = total.astype(BF16)
            for d in (2, 1, 3):
                y_copy(part, k, d).start()

    def section_sum(part, k):
        for d in (1, 2, 3):
            y_copy(part, k, d).wait()
        total = p_own[k, pl.ds(pl.multiple_of(part * 64 + y * 16, 16), 16), :]
        for d in range(3):
            total += y_recv[part, k, d].astype(F32)
        return total

    def z_copy(k):
        return remote(z_send.at[k], z_recv.at[k], zs_send.at[k], zs_recv.at[k], opposite)

    def f_copy(k, cc):
        return remote(
            f_send.at[k, cc], f_recv.at[k, core], fs_send.at[k, cc], fs_recv.at[k, core], (after, at(y, 1 - near, cc))
        )

    pair_sum(0)

    def mixer_forward():
        for name in ("raw", "bias", "decay", "b", "c", "x", "z", "skip", "gain"):
            loads[name].wait()
        pads[...] = jnp.zeros_like(pads)
        pads[1, :HEADS, :] = raw[...].astype(F32)
        pads[0] = pads[1].T
        pads[0, :, :HEADS] += bias[...]
        pads[2, :, :HEADS] = jnp.broadcast_to(decay[...], (TOKENS, HEADS))
        stepped = pads[0]
        size = jnp.maximum(stepped, 0.0) + jnp.log1p(jnp.exp(-jnp.abs(stepped)))
        rate = -jnp.exp(pads[2])
        pads[1] = size
        pads[2] = rate
        row, col = iota((TOKENS, TOKENS), 0), iota((TOKENS, TOKENS), 1)
        lower = jnp.where(row >= col, 1.0, 0.0)
        cumulated = nn(lower, size * rate, HIGHEST)
        cumulated_t = cumulated.T
        size_t = size.T
        g_table[...] = nt(c_in[...], b[...])
        table = g_table[...]
        lane = iota((TOKENS, 128), 1)
        head_of = jnp.where(iota((8, CHANNELS), 1) // HEAD_DIM == iota((8, CHANNELS), 0), 1.0, 0.0)
        skip_row = nn(jnp.broadcast_to(skip[...], (8, HEADS)), head_of, HIGHEST)[:1]
        for pair in range(HEADS // 2):
            cols = slice(pair * 128, pair * 128 + 128)
            xp = x[:, cols].astype(F32)
            x_stack[pair, :TOKENS] = jnp.where(lane < HEAD_DIM, xp, 0.0).astype(BF16)
            x_stack[pair, TOKENS:] = jnp.where(lane < HEAD_DIM, 0.0, xp).astype(BF16)
            ws = []
            for j in range(2):
                h = pair * 2 + j
                spread = cumulated[:, h : h + 1] - cumulated_t[h : h + 1, :]
                e = jnp.exp(jnp.where(row >= col, spread, -1e30)) * size_t[h : h + 1, :]
                ed[h] = e
                w = e * table
                w_t[pair, :, j * TOKENS : (j + 1) * TOKENS] = w.T.astype(BF16)
                ws.append(w.astype(BF16))
            y_val[:, cols] = nn(jnp.concatenate(ws, axis=1), x_stack[pair]) + skip_row[:, cols] * xp
        zf = z[...].astype(F32)
        sig = 1.0 / (1.0 + jnp.exp(-zf))
        silu = zf * sig
        gated = y_val[...] * silu
        r = lax.rsqrt(jnp.mean(gated * gated, axis=1, keepdims=True) + EPSILON)
        normed[...] = gated * r
        s_gate[...] = silu * r
        q_gate[...] = y_val[...] * (sig + silu * (1.0 - sig)) * r

    mixer_forward()

    for k in range(PARTS):
        total = section_sum(0, k)
        z_send[k] = total.astype(BF16)
        pl.when(late & (swaps_out == 1))(z_copy(k).start)
        for cc in range(2):
            f_send[k, cc] = fold(total[cc * ROWS : (cc + 1) * ROWS]).astype(BF16)
            pl.when(forwards * (1 - first * (1 - near)) == 1)(f_copy(k, cc).start)
    pair_sum(1)

    def hand_on(i):
        for d in (2, 1, 3):
            y_gather(i, d).start()
        sib_gather(i, 0).start()

    def hand_over(i):
        for d in (1, 3, 2):
            arrived(slot(i, d, core))
            sib_gather(i, d).start()

    @pl.when(z_hi == 0)
    def _():
        pl.when(readied[0] > 0)(lambda: pl.semaphore_wait(ready.at[0], readied[0]))
        pl.when(at_start == 1)(gather_copy(0).start)

    pl.when(first + from_end == 1)(lambda: arrived(slot(0, 0, core)))
    hand_on(0)

    @pl.when(z_hi == 0)
    def _():
        pl.semaphore_wait(ready.at[1], readied[1])
        for k in range(PARTS):
            pl.when(swaps_out == 1)(z_copy(k).start)
            for cc in range(2):
                pl.when(forwards * (1 - near) == 1)(f_copy(k, cc).start)
        pl.when(sends_far == 1)(gather_copy(1).start)
        pl.when(forwards == 1)(forward_copy().start)

    for k in range(PARTS):
        r_sum[k] = section_sum(1, k)

    def n_copy(k, cc):
        return remote(
            n_send.at[k, cc], n_recv.at[k, core], ns_send.at[k, cc], ns_recv.at[k, core], (after, at(y, near, cc))
        )

    def produce():
        for k in range(PARTS):
            pl.when(swaps_out == 1)(z_copy(k).wait_send)

            @pl.when(swaps_in == 1)
            def _(k=k):
                z_copy(k).wait_recv()
                r_sum[k] += z_recv[k].astype(F32)

            total = r_sum[k]
            for cc in range(2):
                n_send[k, cc] = fold(total[cc * ROWS : (cc + 1) * ROWS]).astype(BF16)
                n_copy(k, cc).start()

    pl.when(swaps_in == 0)(produce)
    hand_over(0)
    pl.when(late & (swaps_in == 1))(produce)
    arrived(slot(1, 0, core))
    hand_on(1)
    hand_over(1)
    pl.when(first * swaps_in == 1)(produce)

    for i in range(2):
        for d in range(4):
            arrived(slot(i, d, 1 - core))
    for m in range(8):
        first, second = gathered[2 * m].astype(F32), gathered[2 * m + 1].astype(F32)
        for j in range(2):
            part = jnp.concatenate([first[j * 8 : j * 8 + 8], second[j * 8 : j * 8 + 8]], axis=0)
            rows_in[m * 16 : m * 16 + 16, j * HALF : (j + 1) * HALF] = part.astype(BF16)
    fed = jnp.where(p == n_pipe - 1, 0.0, 1.0)
    cotangent = nt(rows_in[...], weight[...]) * (scale * fed)

    n_val = normed[...]
    cn = cotangent * n_val
    ggain[...] = jnp.sum(cn, axis=0, keepdims=True)
    inner = jnp.mean(cn * gain[...], axis=1, keepdims=True)
    base = cotangent * gain[...] - n_val * inner
    gz[0] = (base * q_gate[...]).astype(BF16)
    dy = base * s_gate[...]
    head_cols = jnp.where(iota((CHANNELS, 128), 0) // HEAD_DIM == iota((CHANNELS, 128), 1), 1.0, 0.0)
    skip_cols = jnp.sum(dy * x[...].astype(F32), axis=0, keepdims=True)
    gskip[...] = nn(jnp.broadcast_to(skip_cols, (8, CHANNELS)), head_cols, HIGHEST)[:1, :HEADS]
    head_of = jnp.where(iota((8, CHANNELS), 1) // HEAD_DIM == iota((8, CHANNELS), 0), 1.0, 0.0)
    skip_row = nn(jnp.broadcast_to(skip[...], (8, HEADS)), head_of, HIGHEST)[:1]
    table = g_table[...]
    lane = iota((TOKENS, 128), 1)
    sub = iota((128, TOKENS), 0)
    d_table = jnp.zeros((TOKENS, TOKENS), F32)
    row_sums = jnp.zeros((TOKENS, 128), F32)
    col_sums = jnp.zeros((128, TOKENS), F32)
    for pair in range(HEADS // 2):
        cols = slice(pair * 128, pair * 128 + 128)
        dyp = dy[:, cols]
        d_w = nt(dyp.astype(BF16), x_stack[pair])
        stack = jnp.concatenate(
            [jnp.where(lane < HEAD_DIM, dyp, 0.0), jnp.where(lane < HEAD_DIM, 0.0, dyp)], axis=0
        ).astype(BF16)
        gx[0, :, cols] = (nn(w_t[pair], stack) + skip_row[:, cols] * dyp).astype(BF16)
        for j in range(2):
            h = pair * 2 + j
            t_h = d_w[:, j * TOKENS : (j + 1) * TOKENS] * ed[h]
            d_table += t_h
            s_h = t_h * table
            row_sums = jnp.where(lane == h, jnp.sum(s_h, axis=1, keepdims=True), row_sums)
            col_sums = jnp.where(sub == h, jnp.sum(s_h, axis=0, keepdims=True), col_sums)
    gc[0] = nn(d_table.astype(BF16), b[...]).astype(BF16)
    gb[0] = nn(d_table.T.astype(BF16), c_in[...]).astype(BF16)
    direct = col_sums.T
    row, col = iota((TOKENS, TOKENS), 0), iota((TOKENS, TOKENS), 1)
    upper = jnp.where(col >= row, 1.0, 0.0)
    carried = nn(upper, row_sums - direct, HIGHEST)
    size, rate = pads[1], pads[2]
    d_size = direct / size + rate * carried
    d_step = d_size / (1.0 + jnp.exp(-pads[0]))
    gstep[0] = d_step.T[:HEADS].astype(BF16)
    gbias[...] = jnp.sum(d_step, axis=0, keepdims=True)[:, :HEADS]
    gdecay[...] = jnp.sum(size * rate * carried, axis=0, keepdims=True)[:, :HEADS]

    held = jnp.where(p == 0, 0.0, 1.0)
    for k in range(PARTS):
        for cc in range(2):
            remote(
                n_send.at[k, 0], n_recv.at[k, cc], ns_send.at[k, 0], ns_recv.at[k, cc], sibling
            ).wait_recv()

            def keep(got, start=cc * HALF + k * WIDTH):
                got = got * held
                arriving[0, :, start : start + WIDTH // 2] = got[:8].astype(BF16)
                arriving[0, :, start + WIDTH // 2 : start + WIDTH] = got[8:].astype(BF16)

            @pl.when(gets_sum == 1)
            def _(k=k, cc=cc, keep=keep):
                remote(
                    f_send.at[k, 0], f_recv.at[k, cc], fs_send.at[k, 0], fs_recv.at[k, cc], sibling
                ).wait_recv()
                keep(n_recv[k, cc].astype(F32) + f_recv[k, cc].astype(F32))

            pl.when(gets_sum == 0)(lambda k=k, cc=cc, keep=keep: keep(n_recv[k, cc].astype(F32)))

    gather_copy(0).wait_send()
    pl.when(sends_far == 1)(gather_copy(1).wait_send)
    pl.when(forwards == 1)(forward_copy().wait_send)
    for i in range(2):
        for d in (1, 2, 3):
            y_gather(i, d).wait_send()
        for d in range(4):
            sib_gather(i, d).wait_send()
    for k in range(PARTS):
        for cc in range(2):
            n_copy(k, cc).wait_send()
            pl.when(forwards == 1)(f_copy(k, cc).wait_send)


def store_all(*refs):
    sem = refs[-1]
    copies = [pltpu.make_async_copy(refs[i], refs[10 + i], sem.at[i]) for i in range(10)]
    for copy in copies:
        copy.start()
    for copy in copies:
        copy.wait()


def solution(mesh):
    in_specs = (
        P("pipe", None, "tp"),
        P("pipe", "tp", None),
        P("pipe", "tp", None),
        P("pipe", "tp"),
        P("pipe", None, "tp"),
        P("pipe", None, "tp"),
        P("pipe", None, "tp"),
        P("pipe", None, "tp"),
        P("pipe", None, "tp"),
        P("pipe", "tp"),
        P("pipe", "tp"),
        P("pipe", "tp"),
        P("pipe", "tp"),
        P("pipe", "tp", None),
    )
    out_specs = (
        P("pipe", "tp", None),
        P("pipe", None, "tp"),
        P("pipe", None, "tp"),
        P("pipe", None, "tp"),
        P("pipe", None, "tp"),
        P("pipe", None, "tp"),
        P("pipe", "tp"),
        P("pipe", "tp"),
        P("pipe", "tp"),
        P("pipe", "tp"),
    )
    out_shape = [
        jax.ShapeDtypeStruct(shape, dtype)
        for shape, dtype in (
            ((1, ROWS, D), BF16),
            ((1, TOKENS, CHANNELS), BF16),
            ((1, TOKENS, CHANNELS), BF16),
            ((1, TOKENS, STATE), BF16),
            ((1, TOKENS, STATE), BF16),
            ((1, HEADS, TOKENS), BF16),
            ((1, HEADS), F32),
            ((1, HEADS), F32),
            ((1, HEADS), F32),
            ((1, CHANNELS), F32),
        )
    ]
    vmem = pltpu.VMEM
    dma = pltpu.SemaphoreType.DMA
    scratch = [
        vmem((TOKENS, CHANNELS), BF16), vmem((ROWS, D), BF16), vmem((CHANNELS, D), BF16), vmem((1, 16), jnp.int32),
        vmem((TOKENS, CHANNELS), BF16), vmem((TOKENS, CHANNELS), BF16), vmem((TOKENS, STATE), BF16),
        vmem((TOKENS, STATE), BF16), vmem((HEADS, TOKENS), BF16), vmem((1, HEADS), F32), vmem((1, HEADS), F32),
        vmem((1, HEADS), F32), vmem((1, CHANNELS), F32), vmem((ROWS, D), BF16),
        vmem((16, HALF), BF16), vmem((16, 16, HALF), BF16), vmem((TOKENS, D), BF16), vmem((TOKENS, CHANNELS), BF16),
        vmem((TOKENS, WIDTH), F32), vmem((PARTS, TOKENS, WIDTH), BF16), vmem((PARTS, TOKENS, WIDTH), F32),
        vmem((PARTS, TOKENS, WIDTH), BF16), vmem((PARTS, TOKENS, WIDTH), BF16), vmem((2, PARTS, 3, 16, WIDTH), BF16),
        vmem((PARTS, 16, WIDTH), F32), vmem((PARTS, 16, WIDTH), BF16), vmem((PARTS, 16, WIDTH), BF16),
        vmem((PARTS, 2, 16, WIDTH // 2), BF16), vmem((PARTS, 2, 16, WIDTH // 2), BF16),
        vmem((PARTS, 2, 16, WIDTH // 2), BF16), vmem((PARTS, 2, 16, WIDTH // 2), BF16),
        vmem((3, TOKENS, 128), F32), vmem((HEADS, TOKENS, TOKENS), F32), vmem((HEADS // 2, TOKENS, 2 * TOKENS), BF16),
        vmem((HEADS // 2, 2 * TOKENS, 128), BF16), vmem((TOKENS, TOKENS), F32), vmem((TOKENS, CHANNELS), F32),
        vmem((TOKENS, CHANNELS), F32), vmem((TOKENS, CHANNELS), F32), vmem((TOKENS, CHANNELS), F32),
        dma((13,)), dma((2, PARTS)), pltpu.SemaphoreType.REGULAR((2,)), dma((17,)), dma((16,)), dma((2, PARTS)), dma((2, PARTS)),
        dma((2, PARTS, 3)), dma((2, PARTS, 3)), dma((PARTS,)), dma((PARTS,)), dma((PARTS, 2)), dma((PARTS, 2)),
        dma((PARTS, 2)), dma((PARTS, 2)),
    ]
    in_hbm = pl.BlockSpec(memory_space=pltpu.HBM)
    in_vmem = pl.BlockSpec(memory_space=pltpu.VMEM)
    call = pl.pallas_call(
        kernel,
        out_shape=[pltpu.VMEM(out.shape, out.dtype) for out in out_shape],
        in_specs=[in_hbm] * 14,
        out_specs=[in_vmem] * 10,
        scratch_shapes=scratch,
        compiler_params=pltpu.CompilerParams(
            collective_id=0, has_side_effects=True, vmem_limit_bytes=48 * 1024 * 1024
        ),
        cost_estimate=pl.CostEstimate(flops=1_200_000_000, bytes_accessed=6_000_000, transcendentals=500_000),
    )

    hand_out = pl.pallas_call(
        store_all,
        out_shape=out_shape,
        in_specs=[in_vmem] * 10,
        out_specs=[in_hbm] * 10,
        scratch_shapes=[dma((10,))],
        cost_estimate=pl.CostEstimate(flops=0, bytes_accessed=900_000, transcendentals=0),
    )

    def on_device(*blocks):
        blocks = list(blocks)
        blocks[8] = jnp.swapaxes(blocks[8], 1, 2)
        blocks = [pltpu.with_memory_space_constraint(block, pltpu.HBM) for block in blocks]
        held = [pltpu.with_memory_space_constraint(result, pltpu.VMEM) for result in call(*blocks)]
        results = list(hand_out(*held))
        results[5] = jnp.swapaxes(results[5], 1, 2)
        return tuple(results)

    return jax.shard_map(on_device, mesh=mesh, in_specs=in_specs, out_specs=out_specs, check_vma=False)
```

```python
import jax
import jax.numpy as jnp
from jax import lax
from jax.experimental import pallas as pl
from jax.experimental.pallas import tpu as pltpu
from jax.sharding import PartitionSpec as P

MESH = pl.DeviceIdType.MESH
HIGHEST = lax.Precision.HIGHEST
F32 = jnp.float32
BF16 = jnp.bfloat16

TOKENS = 128
D = 4096
HALF = D // 2
CHANNELS = 512
HEADS = 8
HEAD_DIM = 64
STATE = 128
ROWS = 8
SCALE_BLOCK = 32
Z_RUN = 8
EPSILON = 1e-05
PARTS = 2
WIDTH = HALF // PARTS


def nt(a, b, precision=None):
    return lax.dot_general(
        a, b, (((1,), (1,)), ((), ())), preferred_element_type=F32, precision=precision
    )


def nn(a, b, precision=None):
    return jnp.dot(a, b, preferred_element_type=F32, precision=precision)


def fold(v):
    n = v.shape[1] // 2
    return jnp.concatenate([v[:, :n], v[:, n:]], axis=0)


def block_scale(exponents):
    depth_left = 127 - exponents
    factor = jnp.ones(exponents.shape, F32)
    for position in range(7):
        switched = ((depth_left >> position) & 1) == 1
        factor = factor * jnp.where(switched, F32(0.5 ** 2**position), F32(1.0))
    return factor


def iota(shape, dim):
    return lax.broadcasted_iota(jnp.int32, shape, dim)


def kernel(
    mixed_hbm, resid_hbm, weight_hbm, exps_hbm, x_hbm, z_hbm, b_hbm, c_hbm, raw_hbm,
    bias_hbm, decay_hbm, skip_hbm, gain_hbm, up_hbm,
    arriving, gx, gz, gb, gc, gstep, gbias, gdecay, gskip, ggain,
    mixed, resid, weight, exps, x, z, b, c_in, raw, bias, decay, skip, gain, up,
    up_send, gathered, rows_in, scaled, temp, p_send, p_own, s_recv, q_send, y_recv, r_sum, z_send, z_recv, n_send, n_recv, f_send, f_recv,
    pads, ed, w_t, x_stack, g_table, y_val, normed, q_gate, s_gate,
    load_sem, w_sem, ready, ag_send, ag_recv, sib_send, sib_recv, ys_send, ys_recv, zs_send, zs_recv, ns_send, ns_recv, fs_send, fs_recv,
):
    p, t = lax.axis_index("pipe"), lax.axis_index("tp")
    n_pipe = lax.axis_size("pipe")
    z_lo = p % Z_RUN
    y, z_hi, core = t // 4, (t // 2) % 2, t % 2
    after, before = (p + 1) % n_pipe, (p + n_pipe - 1) % n_pipe
    turn_up = jnp.where(z_lo == Z_RUN - 1, 1, 0)
    turn_down = jnp.where(z_lo == 0, 1, 0)
    near = (z_hi + turn_up) % 2
    near_down = (z_hi + turn_down) % 2
    late = z_hi == 1

    def at(yy, zz, cc):
        return yy * 4 + zz * 2 + cc

    sibling = (p, at(y, z_hi, 1 - core))
    y_peer = [(p, at((y + d) % 4, z_hi, core)) for d in range(4)]
    opposite = (p, at(y, 1 - z_hi, core))

    def load(i, src, dst):
        return pltpu.make_async_copy(src, dst, load_sem.at[i])

    loads = {
        name: load(i, src.at[0] if len(src.shape) == 3 else src, dst)
        for i, (name, src, dst) in enumerate(
            (
                ("up", up_hbm, up), ("mixed", mixed_hbm, mixed), ("exps", exps_hbm, exps), ("resid", resid_hbm, resid),
                ("raw", raw_hbm, raw), ("bias", bias_hbm, bias), ("decay", decay_hbm, decay),
                ("b", b_hbm, b), ("c", c_hbm, c_in), ("x", x_hbm, x), ("z", z_hbm, z),
                ("skip", skip_hbm, skip), ("gain", gain_hbm, gain),
            )
        )
    }

    def columns(side, k):
        half = 1 - core if side == 0 else core
        return pl.ds(pl.multiple_of(half * HALF + k * WIDTH, WIDTH), WIDTH)

    def w_load(side, k):
        cols = columns(side, k)
        return pltpu.make_async_copy(weight_hbm.at[0, :, cols], weight.at[:, cols], w_sem.at[side, k])

    loads["up"].start()

    def flag(condition):
        return jnp.where(condition, 1, 0)

    far_down = 1 - near_down
    odd = z_lo % 2
    first = flag(z_hi == 0)
    at_start = first * turn_down
    at_half = first * turn_up
    from_half = (1 - first) * turn_down
    from_end = (1 - first) * turn_up
    sends_far = odd + at_start
    gets_far = (1 - odd) + at_half
    forwards = odd * (1 - from_end)
    swaps_out = 1 - forwards
    swaps_in = (1 - odd) + at_half
    gets_sum = (1 - odd) * (1 - from_half)
    partners = [(device, 1, 0, 1, 0, 0) for device in (sibling, *y_peer[1:])]
    partners += [
        (opposite, 1, first, 1, 1 - first, 1),
        ((after, at(y, near, core)), 1, at_half, 1, from_end, 0),
        ((after, at(y, near, 1 - core)), 1, at_half, 0, 0, 0),
        ((after, at(y, 1 - near, core)), forwards, first * (1 - near), gets_far, near, 1),
        ((after, at(y, 1 - near, 1 - core)), forwards, first * (1 - near), 0, 0, 1),
        ((before, at(y, near_down, core)), 1, at_start, 1, from_half, 0),
        ((before, at(y, near_down, 1 - core)), 0, 0, 1, from_half, 0),
        ((before, at(y, far_down, core)), sends_far, first, gets_sum, (1 - first) * (1 - far_down), 1),
        ((before, at(y, far_down, 1 - core)), 0, 0, gets_sum, (1 - first) * (1 - far_down), 1),
    ]
    barrier = pltpu.get_barrier_semaphore()

    def tell(semaphore, device):
        pl.semaphore_signal(semaphore, inc=1, device_id=device, device_id_type=MESH)

    greeted, readied = 0, [0, 0]
    for device, to_it, to_held, from_it, from_held, which in partners:
        greet = from_it * (1 - from_held) + to_it * to_held
        pl.when(greet > 0)(lambda device=device: tell(barrier, device))
        greeted += flag(to_it * (1 - to_held) + from_it * from_held > 0)
        readied[which] += to_it * to_held

    for name in ("mixed", "exps", "resid"):
        loads[name].start()
    for k in range(PARTS):
        for side in range(2):
            w_load(side, k).start()
    for name in ("raw", "bias", "decay", "b", "c", "x", "z", "skip", "gain"):
        loads[name].start()

    def remote(src, dst, send, recv, device):
        return pltpu.make_async_remote_copy(
            src_ref=src, dst_ref=dst, send_sem=send, recv_sem=recv, device_id=device, device_id_type=MESH
        )

    loads["up"].wait()
    up_send[...] = fold(up[...].astype(F32)).astype(BF16)

    def gather_copy(i):
        device = (before, at(y, near_down if i == 0 else far_down, core))
        return remote(up_send, gathered.at[t], ag_send.at[i], ag_recv.at[t], device)

    def enter():
        pl.semaphore_wait(barrier, greeted)
        pl.when(sends_far * z_hi == 1)(gather_copy(1).start)
        pl.when(at_start == 0)(gather_copy(0).start)
        for device, _, _, from_it, from_held, which in partners:
            pl.when(from_it * from_held == 1)(lambda device=device, which=which: tell(ready.at[which], device))

    pl.when(late)(enter)

    def slot(i, d, cc):
        return at((y + d) % 4, near if i == 0 else 1 - near, cc)

    def block_copy(i, d, device, send):
        s = slot(i, d, core)
        return remote(gathered.at[s], gathered.at[s], send, ag_recv.at[s], device)

    def y_gather(i, d):
        return block_copy(i, 0, y_peer[d], ag_send.at[2 + i * 3 + d - 1])

    def sib_gather(i, d):
        return block_copy(i, d, sibling, ag_send.at[8 + i * 4 + d])

    def arrived(s):
        remote(gathered.at[s], gathered.at[s], ag_send.at[0], ag_recv.at[s], sibling).wait_recv()

    loads["mixed"].wait()
    loads["exps"].wait()
    loads["resid"].wait()
    expand = jnp.where(iota((16, CHANNELS), 1) // SCALE_BLOCK == iota((16, CHANNELS), 0), 1.0, 0.0).astype(BF16)
    scale = nn(jnp.broadcast_to(block_scale(exps[...]), (8, 16)).astype(BF16), expand)[:1]
    for part in range(2):
        for yy in range(4):
            rows = pl.ds(pl.multiple_of(yy * 32 + (1 - near if part == 0 else near) * 16, 16), 16)
            scaled[part * 64 + yy * 16 : part * 64 + yy * 16 + 16] = (mixed[rows].astype(F32) * scale).astype(BF16)
    mine = pl.ds(pl.multiple_of((1 - turn_up) * 64 + y * 16 + core * ROWS, ROWS), ROWS)

    def sib_copy(part, k):
        rows = pl.ds(part * 64, 64)
        return remote(p_send.at[k, rows], s_recv.at[k, rows], sib_send.at[part, k], sib_recv.at[part, k], sibling)

    for k in range(PARTS):
        for side in range(2):
            w_load(side, k).wait()
            target = temp if side == 0 else p_own.at[k]
            cols = columns(side, k)
            target[...] = nn(scaled[...], weight[:, cols])
            target[mine, :] += resid[:, cols].astype(F32)
            if side == 0:
                p_send[k] = temp[...].astype(BF16)
                for part in range(2):
                    pl.when(late)(sib_copy(part, k).start)

    def forward_copy():
        return block_copy(0, 0, opposite, ag_send.at[16])

    @pl.when((1 - first) * (1 - from_end) == 1)
    def _():
        arrived(slot(0, 0, core))
        pl.when(forwards == 1)(forward_copy().start)

    @pl.when(z_hi == 0)
    def _():
        enter()
        for part in range(2):
            for k in range(PARTS):
                sib_copy(part, k).start()

    def y_copy(part, k, d):
        to = (y + d) % 4
        return remote(
            q_send.at[k, pl.ds(pl.multiple_of(part * 64 + to * 16, 16), 16)], y_recv.at[part, k, d - 1],
            ys_send.at[part, k, d - 1], ys_recv.at[part, k, d - 1], y_peer[d],
        )

    def pair_sum(part):
        rows = slice(part * 64, part * 64 + 64)
        for k in range(PARTS):
            sib_copy(part, k).wait()
            total = p_own[k, rows] + s_recv[k, rows].astype(F32)
            p_own[k, rows] = total
            q_send[k, rows] = total.astype(BF16)
            for d in (2, 1, 3):
                y_copy(part, k, d).start()

    def section_sum(part, k):
        for d in (1, 2, 3):
            y_copy(part, k, d).wait()
        total = p_own[k, pl.ds(pl.multiple_of(part * 64 + y * 16, 16), 16), :]
        for d in range(3):
            total += y_recv[part, k, d].astype(F32)
        return total

    def z_copy(k):
        return remote(z_send.at[k], z_recv.at[k], zs_send.at[k], zs_recv.at[k], opposite)

    def f_copy(k, cc):
        return remote(
            f_send.at[k, cc], f_recv.at[k, core], fs_send.at[k, cc], fs_recv.at[k, core], (after, at(y, 1 - near, cc))
        )

    pair_sum(0)

    def mixer_forward():
        for name in ("raw", "bias", "decay", "b", "c", "x", "z", "skip", "gain"):
            loads[name].wait()
        pads[...] = jnp.zeros_like(pads)
        pads[1, :HEADS, :] = raw[...].astype(F32)
        pads[0] = pads[1].T
        pads[0, :, :HEADS] += bias[...]
        pads[2, :, :HEADS] = jnp.broadcast_to(decay[...], (TOKENS, HEADS))
        stepped = pads[0]
        size = jnp.maximum(stepped, 0.0) + jnp.log1p(jnp.exp(-jnp.abs(stepped)))
        rate = -jnp.exp(pads[2])
        pads[1] = size
        pads[2] = rate
        row, col = iota((TOKENS, TOKENS), 0), iota((TOKENS, TOKENS), 1)
        lower = jnp.where(row >= col, 1.0, 0.0)
        cumulated = nn(lower, size * rate, HIGHEST)
        cumulated_t = cumulated.T
        size_t = size.T
        g_table[...] = nt(c_in[...], b[...])
        table = g_table[...]
        lane = iota((TOKENS, 128), 1)
        head_of = jnp.where(iota((8, CHANNELS), 1) // HEAD_DIM == iota((8, CHANNELS), 0), 1.0, 0.0)
        skip_row = nn(jnp.broadcast_to(skip[...], (8, HEADS)), head_of, HIGHEST)[:1]
        for pair in range(HEADS // 2):
            cols = slice(pair * 128, pair * 128 + 128)
            xp = x[:, cols].astype(F32)
            x_stack[pair, :TOKENS] = jnp.where(lane < HEAD_DIM, xp, 0.0).astype(BF16)
            x_stack[pair, TOKENS:] = jnp.where(lane < HEAD_DIM, 0.0, xp).astype(BF16)
            ws = []
            for j in range(2):
                h = pair * 2 + j
                spread = cumulated[:, h : h + 1] - cumulated_t[h : h + 1, :]
                e = jnp.exp(jnp.where(row >= col, spread, -1e30)) * size_t[h : h + 1, :]
                ed[h] = e
                w = e * table
                w_t[pair, :, j * TOKENS : (j + 1) * TOKENS] = w.T.astype(BF16)
                ws.append(w.astype(BF16))
            y_val[:, cols] = nn(jnp.concatenate(ws, axis=1), x_stack[pair]) + skip_row[:, cols] * xp
        zf = z[...].astype(F32)
        sig = 1.0 / (1.0 + jnp.exp(-zf))
        silu = zf * sig
        gated = y_val[...] * silu
        r = lax.rsqrt(jnp.mean(gated * gated, axis=1, keepdims=True) + EPSILON)
        normed[...] = gated * r
        s_gate[...] = silu * r
        q_gate[...] = y_val[...] * (sig + silu * (1.0 - sig)) * r

    mixer_forward()

    for k in range(PARTS):
        total = section_sum(0, k)
        z_send[k] = total.astype(BF16)
        pl.when(late & (swaps_out == 1))(z_copy(k).start)
        for cc in range(2):
            f_send[k, cc] = fold(total[cc * ROWS : (cc + 1) * ROWS]).astype(BF16)
            pl.when(forwards * (1 - first * (1 - near)) == 1)(f_copy(k, cc).start)
    pair_sum(1)

    def hand_on(i):
        for d in (2, 1, 3):
            y_gather(i, d).start()
        sib_gather(i, 0).start()

    def hand_over(i):
        for d in (1, 3, 2):
            arrived(slot(i, d, core))
            sib_gather(i, d).start()

    @pl.when(z_hi == 0)
    def _():
        pl.when(readied[0] > 0)(lambda: pl.semaphore_wait(ready.at[0], readied[0]))
        pl.when(at_start == 1)(gather_copy(0).start)

    pl.when(first + from_end == 1)(lambda: arrived(slot(0, 0, core)))
    hand_on(0)

    @pl.when(z_hi == 0)
    def _():
        pl.semaphore_wait(ready.at[1], readied[1])
        pl.when(sends_far == 1)(gather_copy(1).start)
        pl.when(forwards == 1)(forward_copy().start)

    for k in range(PARTS):
        r_sum[k] = section_sum(1, k)

    def n_copy(k, cc):
        return remote(
            n_send.at[k, cc], n_recv.at[k, core], ns_send.at[k, cc], ns_recv.at[k, core], (after, at(y, near, cc))
        )

    def produce():
        for k in range(PARTS):
            pl.when(swaps_out == 1)(z_copy(k).wait_send)

            @pl.when(swaps_in == 1)
            def _(k=k):
                z_copy(k).wait_recv()
                r_sum[k] += z_recv[k].astype(F32)

            total = r_sum[k]
            for cc in range(2):
                n_send[k, cc] = fold(total[cc * ROWS : (cc + 1) * ROWS]).astype(BF16)
                n_copy(k, cc).start()

    pl.when(swaps_in == 0)(produce)
    hand_over(0)
    @pl.when(z_hi == 0)
    def _():
        for k in range(PARTS):
            pl.when(swaps_out == 1)(z_copy(k).start)
            for cc in range(2):
                pl.when(forwards * (1 - near) == 1)(f_copy(k, cc).start)

    arrived(slot(1, 0, core))
    hand_on(1)
    hand_over(1)
    pl.when(swaps_in == 1)(produce)

    for i in range(2):
        for d in range(4):
            arrived(slot(i, d, 1 - core))
    for m in range(8):
        lower, upper = gathered[2 * m].astype(F32), gathered[2 * m + 1].astype(F32)
        for j in range(2):
            part = jnp.concatenate([lower[j * 8 : j * 8 + 8], upper[j * 8 : j * 8 + 8]], axis=0)
            rows_in[m * 16 : m * 16 + 16, j * HALF : (j + 1) * HALF] = part.astype(BF16)
    fed = jnp.where(p == n_pipe - 1, 0.0, 1.0)
    cotangent = nt(rows_in[...], weight[...]) * (scale * fed)

    n_val = normed[...]
    cn = cotangent * n_val
    ggain[...] = jnp.sum(cn, axis=0, keepdims=True)
    inner = jnp.mean(cn * gain[...], axis=1, keepdims=True)
    base = cotangent * gain[...] - n_val * inner
    gz[0] = (base * q_gate[...]).astype(BF16)
    dy = base * s_gate[...]
    head_cols = jnp.where(iota((CHANNELS, 128), 0) // HEAD_DIM == iota((CHANNELS, 128), 1), 1.0, 0.0)
    skip_cols = jnp.sum(dy * x[...].astype(F32), axis=0, keepdims=True)
    gskip[...] = nn(jnp.broadcast_to(skip_cols, (8, CHANNELS)), head_cols, HIGHEST)[:1, :HEADS]
    head_of = jnp.where(iota((8, CHANNELS), 1) // HEAD_DIM == iota((8, CHANNELS), 0), 1.0, 0.0)
    skip_row = nn(jnp.broadcast_to(skip[...], (8, HEADS)), head_of, HIGHEST)[:1]
    table = g_table[...]
    lane = iota((TOKENS, 128), 1)
    sub = iota((128, TOKENS), 0)
    d_table = jnp.zeros((TOKENS, TOKENS), F32)
    row_sums = jnp.zeros((TOKENS, 128), F32)
    col_sums = jnp.zeros((128, TOKENS), F32)
    for pair in range(HEADS // 2):
        cols = slice(pair * 128, pair * 128 + 128)
        dyp = dy[:, cols]
        d_w = nt(dyp.astype(BF16), x_stack[pair])
        stack = jnp.concatenate(
            [jnp.where(lane < HEAD_DIM, dyp, 0.0), jnp.where(lane < HEAD_DIM, 0.0, dyp)], axis=0
        ).astype(BF16)
        gx[0, :, cols] = (nn(w_t[pair], stack) + skip_row[:, cols] * dyp).astype(BF16)
        for j in range(2):
            h = pair * 2 + j
            t_h = d_w[:, j * TOKENS : (j + 1) * TOKENS] * ed[h]
            d_table += t_h
            s_h = t_h * table
            row_sums = jnp.where(lane == h, jnp.sum(s_h, axis=1, keepdims=True), row_sums)
            col_sums = jnp.where(sub == h, jnp.sum(s_h, axis=0, keepdims=True), col_sums)
    gc[0] = nn(d_table.astype(BF16), b[...]).astype(BF16)
    gb[0] = nn(d_table.T.astype(BF16), c_in[...]).astype(BF16)
    direct = col_sums.T
    row, col = iota((TOKENS, TOKENS), 0), iota((TOKENS, TOKENS), 1)
    upper = jnp.where(col >= row, 1.0, 0.0)
    carried = nn(upper, row_sums - direct, HIGHEST)
    size, rate = pads[1], pads[2]
    d_size = direct / size + rate * carried
    d_step = d_size / (1.0 + jnp.exp(-pads[0]))
    gstep[0] = d_step.T[:HEADS].astype(BF16)
    gbias[...] = jnp.sum(d_step, axis=0, keepdims=True)[:, :HEADS]
    gdecay[...] = jnp.sum(size * rate * carried, axis=0, keepdims=True)[:, :HEADS]

    held = jnp.where(p == 0, 0.0, 1.0)
    for k in range(PARTS):
        for cc in range(2):
            remote(
                n_send.at[k, 0], n_recv.at[k, cc], ns_send.at[k, 0], ns_recv.at[k, cc], sibling
            ).wait_recv()

            def keep(got, start=cc * HALF + k * WIDTH):
                got = got * held
                arriving[0, :, start : start + WIDTH // 2] = got[:8].astype(BF16)
                arriving[0, :, start + WIDTH // 2 : start + WIDTH] = got[8:].astype(BF16)

            @pl.when(gets_sum == 1)
            def _(k=k, cc=cc, keep=keep):
                remote(
                    f_send.at[k, 0], f_recv.at[k, cc], fs_send.at[k, 0], fs_recv.at[k, cc], sibling
                ).wait_recv()
                keep(n_recv[k, cc].astype(F32) + f_recv[k, cc].astype(F32))

            pl.when(gets_sum == 0)(lambda k=k, cc=cc, keep=keep: keep(n_recv[k, cc].astype(F32)))

    gather_copy(0).wait_send()
    pl.when(sends_far == 1)(gather_copy(1).wait_send)
    pl.when(forwards == 1)(forward_copy().wait_send)
    for i in range(2):
        for d in (1, 2, 3):
            y_gather(i, d).wait_send()
        for d in range(4):
            sib_gather(i, d).wait_send()
    for k in range(PARTS):
        for cc in range(2):
            n_copy(k, cc).wait_send()
            pl.when(forwards == 1)(f_copy(k, cc).wait_send)


def store_all(*refs):
    sem = refs[-1]
    copies = [pltpu.make_async_copy(refs[i], refs[10 + i], sem.at[i]) for i in range(10)]
    for copy in copies:
        copy.start()
    for copy in copies:
        copy.wait()


def solution(mesh):
    in_specs = (
        P("pipe", None, "tp"),
        P("pipe", "tp", None),
        P("pipe", "tp", None),
        P("pipe", "tp"),
        P("pipe", None, "tp"),
        P("pipe", None, "tp"),
        P("pipe", None, "tp"),
        P("pipe", None, "tp"),
        P("pipe", None, "tp"),
        P("pipe", "tp"),
        P("pipe", "tp"),
        P("pipe", "tp"),
        P("pipe", "tp"),
        P("pipe", "tp", None),
    )
    out_specs = (
        P("pipe", "tp", None),
        P("pipe", None, "tp"),
        P("pipe", None, "tp"),
        P("pipe", None, "tp"),
        P("pipe", None, "tp"),
        P("pipe", None, "tp"),
        P("pipe", "tp"),
        P("pipe", "tp"),
        P("pipe", "tp"),
        P("pipe", "tp"),
    )
    out_shape = [
        jax.ShapeDtypeStruct(shape, dtype)
        for shape, dtype in (
            ((1, ROWS, D), BF16),
            ((1, TOKENS, CHANNELS), BF16),
            ((1, TOKENS, CHANNELS), BF16),
            ((1, TOKENS, STATE), BF16),
            ((1, TOKENS, STATE), BF16),
            ((1, HEADS, TOKENS), BF16),
            ((1, HEADS), F32),
            ((1, HEADS), F32),
            ((1, HEADS), F32),
            ((1, CHANNELS), F32),
        )
    ]
    vmem = pltpu.VMEM
    dma = pltpu.SemaphoreType.DMA
    scratch = [
        vmem((TOKENS, CHANNELS), BF16), vmem((ROWS, D), BF16), vmem((CHANNELS, D), BF16), vmem((1, 16), jnp.int32),
        vmem((TOKENS, CHANNELS), BF16), vmem((TOKENS, CHANNELS), BF16), vmem((TOKENS, STATE), BF16),
        vmem((TOKENS, STATE), BF16), vmem((HEADS, TOKENS), BF16), vmem((1, HEADS), F32), vmem((1, HEADS), F32),
        vmem((1, HEADS), F32), vmem((1, CHANNELS), F32), vmem((ROWS, D), BF16),
        vmem((16, HALF), BF16), vmem((16, 16, HALF), BF16), vmem((TOKENS, D), BF16), vmem((TOKENS, CHANNELS), BF16),
        vmem((TOKENS, WIDTH), F32), vmem((PARTS, TOKENS, WIDTH), BF16), vmem((PARTS, TOKENS, WIDTH), F32),
        vmem((PARTS, TOKENS, WIDTH), BF16), vmem((PARTS, TOKENS, WIDTH), BF16), vmem((2, PARTS, 3, 16, WIDTH), BF16),
        vmem((PARTS, 16, WIDTH), F32), vmem((PARTS, 16, WIDTH), BF16), vmem((PARTS, 16, WIDTH), BF16),
        vmem((PARTS, 2, 16, WIDTH // 2), BF16), vmem((PARTS, 2, 16, WIDTH // 2), BF16),
        vmem((PARTS, 2, 16, WIDTH // 2), BF16), vmem((PARTS, 2, 16, WIDTH // 2), BF16),
        vmem((3, TOKENS, 128), F32), vmem((HEADS, TOKENS, TOKENS), F32), vmem((HEADS // 2, TOKENS, 2 * TOKENS), BF16),
        vmem((HEADS // 2, 2 * TOKENS, 128), BF16), vmem((TOKENS, TOKENS), F32), vmem((TOKENS, CHANNELS), F32),
        vmem((TOKENS, CHANNELS), F32), vmem((TOKENS, CHANNELS), F32), vmem((TOKENS, CHANNELS), F32),
        dma((13,)), dma((2, PARTS)), pltpu.SemaphoreType.REGULAR((2,)), dma((17,)), dma((16,)), dma((2, PARTS)), dma((2, PARTS)),
        dma((2, PARTS, 3)), dma((2, PARTS, 3)), dma((PARTS,)), dma((PARTS,)), dma((PARTS, 2)), dma((PARTS, 2)),
        dma((PARTS, 2)), dma((PARTS, 2)),
    ]
    in_hbm = pl.BlockSpec(memory_space=pltpu.HBM)
    in_vmem = pl.BlockSpec(memory_space=pltpu.VMEM)
    call = pl.pallas_call(
        kernel,
        out_shape=[pltpu.VMEM(out.shape, out.dtype) for out in out_shape],
        in_specs=[in_hbm] * 14,
        out_specs=[in_vmem] * 10,
        scratch_shapes=scratch,
        compiler_params=pltpu.CompilerParams(
            collective_id=0, has_side_effects=True, vmem_limit_bytes=48 * 1024 * 1024
        ),
        cost_estimate=pl.CostEstimate(flops=1_200_000_000, bytes_accessed=6_000_000, transcendentals=500_000),
    )

    hand_out = pl.pallas_call(
        store_all,
        out_shape=out_shape,
        in_specs=[in_vmem] * 10,
        out_specs=[in_hbm] * 10,
        scratch_shapes=[dma((10,))],
        cost_estimate=pl.CostEstimate(flops=0, bytes_accessed=900_000, transcendentals=0),
    )

    def on_device(*blocks):
        blocks = list(blocks)
        blocks[8] = jnp.swapaxes(blocks[8], 1, 2)
        blocks = [pltpu.with_memory_space_constraint(block, pltpu.HBM) for block in blocks]
        held = [pltpu.with_memory_space_constraint(result, pltpu.VMEM) for result in call(*blocks)]
        results = list(hand_out(*held))
        results[5] = jnp.swapaxes(results[5], 1, 2)
        return tuple(results)

    return jax.shard_map(on_device, mesh=mesh, in_specs=in_specs, out_specs=out_specs, check_vma=False)
```
